256 devices in a mesh: tm: 8 (over y, core), space: 32 (over x, z).
Axes of the slice: x: 4, y: 4, z: 8, core: 2. Of those that a mesh axis runs over, the one named last changes fastest.
Arguments:
- latent: bfloat16 [32, 64, 64, 256], P('tm', 'space'), may hold values from -24 to 24
- clip_frames: int32 [8], replicated, may hold values from 1 to 4, 16 in all
- clip_rank: int32 [8], replicated, may hold values from 0 to 7, each once
- group_of: int32 [256], replicated, may hold values from 0 to 31, as said below
- gain_first: float32 [256], replicated, may hold values from 0.1 to 1.9
- shift_first: float32 [256], replicated, may hold values from -3 to 3
- conv_first: bfloat16 [3, 3, 3, 256, 256], replicated, may hold values from -0.078125 to 0.078125
- bias_first: float32 [256], replicated, may hold values from -3 to 3
- gain_second: float32 [256], replicated, may hold values from 0.1 to 1.9
- shift_second: float32 [256], replicated, may hold values from -3 to 3
- conv_second: bfloat16 [3, 3, 3, 256, 256], replicated, may hold values from -0.078125 to 0.078125
- bias_second: float32 [256], replicated, may hold values from -3 to 3
Outputs:
- decoded: bfloat16 [16, 64, 64, 256], P('tm', 'space')
The draws below stay inside these ranges and needn't reach their ends.
Inputs may be any that keep to these rules, and one draw needn't show every extreme that they name: `clip_frames`: the frame counts sum to 16; some clip has exactly 4 frames. `clip_rank`: each number of 0 to 7 appears once. `group_of`: each group number names exactly 8 channels.
All inputs are finite; a program needn't handle non-finite values.
Results may differ from the reference program's by a relative error of at most 0.0051.
Values may be sent and summed in bfloat16 or wider, within the bound.
No kernel may reach another device: no remote copies, remote signals or barrier semaphores. Data moves between devices by JAX's collectives and lax.ppermute only.
A program may use at most 64 MiB of HBM per device.

```python
import math
import jax
import jax.numpy as jnp
import numpy as np
from jax import lax

C = 256
G = 32
COLS = 64
HOME_F = 4
NCLIP = 8
STREAM = 16
HOMES = 32
H = 64


def draw_latent(key, part):
    key = jax.random.fold_in(key, 11)
    subkeys = jax.random.split(key, 4)
    base_draw = jax.random.truncated_normal(subkeys[0], -3.0, 3.0, (HOMES, H, COLS, C), jnp.float32)
    rough_range = 0.6
    row_trend = 0.5 + jnp.arange(H, dtype=jnp.float32) / (H - 1)
    row_scale = row_trend * jnp.exp(jax.random.uniform(subkeys[1], (H,), jnp.float32, -rough_range, rough_range))
    channel_scale = jnp.exp(jax.random.uniform(subkeys[2], (C,), jnp.float32, -1.15, 1.15))
    frame_scale = jnp.exp(jax.random.uniform(subkeys[3], (HOMES,), jnp.float32, -0.4, 0.4))
    scaled = base_draw * 0.3 * row_scale[None, :, None, None] * channel_scale * frame_scale[:, None, None, None]
    return scaled.astype(jnp.bfloat16)


def draw_group_of(key, part):
    key = jax.random.fold_in(key, 23)
    order = jax.random.permutation(key, C)
    return (order // (C // G)).astype(jnp.int32)


def profile(count, total, limit, skew):
    portions = [(1 << 20) // math.isqrt(rank ** skew) + 1 for rank in range(2, count + 1)]
    surplus, holding = total - limit - (count - 1), [1] * (count - 1)
    while surplus > 0:
        candidates = [i for i in range(count - 1) if holding[i] < limit]
        whole, budget = sum([portions[i] for i in candidates]), surplus
        for i in candidates:
            more = min(limit - holding[i], max(1, budget * portions[i] // whole), surplus)
            holding[i] = holding[i] + more
            surplus = surplus - more
    return np.array([limit] + holding)


def uneven_parts(key, number_of, total, limit, skew):
    if number_of == 2:
        one = jax.random.randint(key, (), max(1, total - limit), min(limit, total - 1) + 1)
        return jnp.stack([one, total - one])
    sizes = jnp.asarray(profile(number_of, total, limit, skew), jnp.int32)
    twos = (number_of - 1) // 2
    giver, sink = sizes[1:1 + 2 * twos:2], sizes[2:2 + 2 * twos:2]
    room = jnp.minimum(giver - 1, limit - sink)
    moved = jax.random.randint(jax.random.fold_in(key, 1), (twos,), 0, 1 << 20) % (room + 1)
    sizes = sizes.at[1:1 + 2 * twos:2].set(giver - moved).at[2:2 + 2 * twos:2].set(sink + moved)
    return sizes[jax.random.permutation(jax.random.fold_in(key, 2), number_of)]


def bell_draw(key, shape, scale, limit, held_as=jnp.bfloat16):
    drawn = jax.random.normal(key, shape, jnp.float32) * scale
    return jnp.minimum(jnp.maximum(drawn, -limit), limit).astype(held_as)


def setup_inputs(seed: int = 0) -> dict:
    seeds = jax.random.split(jax.random.key(seed), 13)
    return {
        "latent": draw_latent(jax.random.fold_in(seeds[12], 71), 0),
        "clip_frames": uneven_parts(seeds[1], NCLIP, STREAM, HOME_F, 2).astype(jnp.int32),
        "clip_rank": jax.random.permutation(seeds[2], NCLIP).astype(jnp.int32),
        "group_of": draw_group_of(jax.random.fold_in(seeds[12], 71), 0),
        "gain_first": jnp.clip(1.0 + 0.18 * jax.random.normal(seeds[4], (C,), jnp.float32), 0.1, 1.9),
        "shift_first": bell_draw(seeds[5], (C,), 0.5, 3.0, jnp.float32),
        "conv_first": bell_draw(seeds[6], (3, 3, 3, C, C), (27 * C) ** -0.5, 0.078125),
        "bias_first": bell_draw(seeds[7], (C,), 0.5, 3.0, jnp.float32),
        "gain_second": jnp.clip(1.0 + 0.18 * jax.random.normal(seeds[8], (C,), jnp.float32), 0.1, 1.9),
        "shift_second": bell_draw(seeds[9], (C,), 0.5, 3.0, jnp.float32),
        "conv_second": bell_draw(seeds[10], (3, 3, 3, C, C), (27 * C) ** -0.5, 0.078125),
        "bias_second": bell_draw(seeds[11], (C,), 0.5, 3.0, jnp.float32),
    }


EPSILON = 1e-06
HIGH = lax.Precision.HIGHEST

def group_table(group_of):
    return (group_of[:, None] == jnp.arange(G, dtype=jnp.int32)[None, :]).astype(jnp.float32)

def normalize(field, live_mask, count, member_groups, gain, shift):
    values = field.astype(jnp.float32)
    weights = live_mask[:, None, None, None]
    sums = jnp.dot(lax.optimization_barrier(jnp.sum(values * weights, axis=(0, 1, 2))), member_groups, precision=HIGH)
    mean_channel = jnp.dot(member_groups, sums / count, precision=HIGH)
    centred = values - mean_channel
    spread = jnp.dot(lax.optimization_barrier(jnp.sum(centred * centred * weights, axis=(0, 1, 2))), member_groups, precision=HIGH) / count
    scale_channel = jnp.dot(member_groups, lax.rsqrt(spread + EPSILON), precision=HIGH)
    return jax.nn.silu(centred * scale_channel * gain + shift).astype(jnp.bfloat16)

def causal_conv(field, kernel, bias):
    frames, height, columns, channels = field.shape
    padded = jnp.pad(field, ((2, 0), (1, 1), (1, 1), (0, 0)), mode='edge')
    summed = jnp.zeros((frames * height * columns, channels), jnp.float32)
    for back_step in range(3):
        for row_step in range(3):
            for col_step in range(3):
                shifted = padded[back_step:back_step + frames, row_step:row_step + height, col_step:col_step + columns]
                summed = summed + jnp.dot(shifted.reshape(-1, channels), kernel[back_step, row_step, col_step], preferred_element_type=jnp.float32)
    return summed.reshape(frames, height, columns, channels) + bias

def reference(latent, clip_frames, clip_rank, group_of, gain_first, shift_first, conv_first, bias_first, gain_second, shift_second, conv_second, bias_second):
    member_groups = group_table(group_of)
    clips = latent.reshape(NCLIP, HOME_F, H, COLS, C)

    def decode_clip(clip_item):
        field, length = clip_item
        live_mask = (jnp.arange(HOME_F, dtype=jnp.int32) < length).astype(jnp.float32)
        count = length.astype(jnp.float32) * float(H * COLS * (C // G))
        first_act = normalize(field, live_mask, count, member_groups, gain_first, shift_first)
        hidden = causal_conv(first_act, conv_first, bias_first).astype(jnp.bfloat16)
        second_act = normalize(hidden, live_mask, count, member_groups, gain_second, shift_second)
        return (field.astype(jnp.float32) + causal_conv(second_act, conv_second, bias_second)).astype(jnp.bfloat16)
    finished = lax.map(decode_clip, (clips, clip_frames))
    lengths = clip_frames
    earlier = (clip_rank[None, :] < clip_rank[:, None]).astype(jnp.int32)
    clip_start = lax.optimization_barrier(jnp.sum(earlier * lengths[None, :], axis=1))
    position = jnp.arange(STREAM, dtype=jnp.int32)
    member = ((position[:, None] >= clip_start[None, :]) & (position[:, None] < (clip_start + lengths)[None, :])).astype(jnp.int32)
    clip_index = lax.optimization_barrier(jnp.sum(member * jnp.arange(NCLIP, dtype=jnp.int32)[None, :], axis=1))
    frame_index = position - lax.optimization_barrier(jnp.sum(member * clip_start[None, :], axis=1))
    source = (clip_index * HOME_F + frame_index).astype(jnp.int32)
    return jnp.take(finished.reshape(HOMES, H, COLS, C), source, axis=0)
```

```python
import functools

import jax
import jax.numpy as jnp
from jax import lax
from jax.experimental import pallas as pl
from jax.experimental.pallas import tpu as pltpu
from jax.sharding import PartitionSpec as P

G = 32
LANES = 128
EPSILON = 1e-06
HIGH = lax.Precision.HIGHEST
F32 = jnp.float32
BF16 = jnp.bfloat16
VMEM = pl.BlockSpec(memory_space=pltpu.VMEM)
SMEM = pl.BlockSpec(memory_space=pltpu.SMEM)
HBM = pl.BlockSpec(memory_space=pl.ANY)
LIMIT = 40 * 1024 * 1024


def dot_high(a, b, contract):
    return lax.dot_general(a, b, ((contract[:1], contract[1:]), ((), ())), precision=HIGH, preferred_element_type=F32)


def member_rows(group_row, first):
    channels = group_row.shape[1]
    rows = lax.broadcasted_iota(jnp.int32, (LANES, channels), 0)
    return (rows - first == group_row).astype(F32)


def clip_start_of(frames_ref, rank_ref, clip):
    start = jnp.int32(0)
    for k in range(frames_ref.shape[0]):
        start = start + jnp.where(rank_ref[k] < rank_ref[clip], frames_ref[k], 0)
    return start


def local_stats(field_ref, length, group_row):
    frames, height, columns, channels = field_ref.shape
    pixels = height * columns
    scale = 1.0 / (length.astype(F32) * float(pixels * (channels // G)))
    live = [jnp.where(f < length, 1.0, 0.0).astype(F32) for f in range(frames)]

    def frame(f):
        return field_ref[f].astype(F32).reshape(pixels, channels)

    total = jnp.zeros((1, channels), F32)
    for f in range(frames):
        total = total + live[f] * jnp.sum(frame(f), axis=0, keepdims=True)
    mean_rows = member_rows(group_row, 0)
    group_mean = dot_high(jnp.broadcast_to(total, (8, channels)), mean_rows, (1, 1)) * scale
    mean = dot_high(group_mean, mean_rows, (1, 0))[:1]
    spread = jnp.zeros((1, channels), F32)
    for f in range(frames):
        centred = frame(f) - mean
        spread = spread + live[f] * jnp.sum(centred * centred, axis=0, keepdims=True)
    group_spread = dot_high(jnp.broadcast_to(spread, (8, channels)), member_rows(group_row, G), (1, 1))
    return (group_mean + group_spread)[:1]


def combine_stats(parts, length, pixels, group_row):
    bands = parts.shape[0]
    channels = group_row.shape[1]
    per_band = length.astype(F32) * float(pixels * (channels // G))
    lane = lax.broadcasted_iota(jnp.int32, (1, LANES), 1)
    sums = jnp.sum(parts, axis=0, keepdims=True)
    mean = sums * (1.0 / bands)
    away = parts - mean
    between = jnp.sum(away * away, axis=0, keepdims=True) * per_band
    spread = jnp.where(lane < G, between, jnp.where(lane < 2 * G, sums, 0.0))
    mean = jnp.where(lane < G, mean, 0.0)
    which = lax.broadcasted_iota(jnp.int32, (8, LANES), 0)
    both = jnp.where(which == 0, mean, spread)
    spread_back = dot_high(both, member_rows(group_row, 0) + member_rows(group_row, G), (1, 0))
    variance = spread_back[1:2] / (per_band * bands)
    return spread_back[:1], lax.rsqrt(variance + EPSILON)


def activate(field_ref, above_ref, below_ref, act_ref, mean, scale, shift):
    frames, height, columns, channels = field_ref.shape
    band = lax.axis_index("space")
    top = band == 0
    bottom = band == lax.axis_size("space") - 1
    for f in range(frames):
        for r in range(height + 2):
            if r == 0:
                value = jnp.where(top, field_ref[f, 0], above_ref[f])
            elif r == height + 1:
                value = jnp.where(bottom, field_ref[f, height - 1], below_ref[f])
            else:
                value = field_ref[f, r - 1]
            half = ((value.astype(F32) - mean) * scale + shift) * 0.5
            act = half * jnp.tanh(half) + half
            left = jnp.concatenate([act[:1], act[:-1]], axis=0)
            right = jnp.concatenate([act[1:], act[-1:]], axis=0)
            for step, taken in enumerate((left, act, right)):
                taken = taken.astype(BF16)
                lanes = slice(step * channels, (step + 1) * channels)
                for place in (0, 1, 2) if f == 0 else (f + 2,):
                    act_ref[place, r, :, lanes] = taken


def convolve(act_ref, weight_ref, sem, kernel_hbm, acc_ref, frames, height):
    columns, width = act_ref.shape[2:]
    rows = frames * height * columns
    for tap in range(9):
        back_step, row_step = divmod(tap, 3)
        pltpu.make_async_copy(kernel_hbm.at[tap], weight_ref.at[tap], sem.at[tap]).wait()
        slab = act_ref[back_step : back_step + frames, row_step : row_step + height].reshape(rows, width)
        part = jnp.dot(slab, weight_ref[tap], preferred_element_type=F32)
        if tap == 0:
            acc_ref[...] = part
        else:
            acc_ref[...] += part


def start_weights(kernel_hbm, weight_ref, sem):
    for tap in range(9):
        pltpu.make_async_copy(kernel_hbm.at[tap], weight_ref.at[tap], sem.at[tap]).start()


def stats_kernel(frames_ref, field_ref, group_ref, parts_ref, first_ref, last_ref):
    length = frames_ref[lax.axis_index("tm")]
    height = field_ref.shape[1]
    first_ref[...] = field_ref[:, 0]
    last_ref[...] = field_ref[:, height - 1]
    row = local_stats(field_ref, length, group_ref[...])
    parts_ref[...] = jnp.broadcast_to(row[None], parts_ref.shape)


def first_kernel(
    frames_ref, parts_ref, field_ref, above_ref, below_ref, group_ref, gain_ref, shift_ref, bias_ref, kernel_hbm,
    hidden_ref, out_parts_ref, first_ref, last_ref,
    weight_ref, act_ref, acc_ref, sem,
):
    start_weights(kernel_hbm, weight_ref, sem)
    frames, height, columns, channels = field_ref.shape
    length = frames_ref[lax.axis_index("tm")]
    mean, inverse = combine_stats(parts_ref[:, 0], length, height * columns, group_ref[...])
    activate(field_ref, above_ref, below_ref, act_ref, mean, inverse * gain_ref[...], shift_ref[...])
    convolve(act_ref, weight_ref, sem, kernel_hbm, acc_ref, frames, height)
    hidden = (acc_ref[...] + bias_ref[...]).astype(BF16).reshape(hidden_ref.shape)
    hidden_ref[...] = hidden
    first_ref[...] = hidden_ref[:, 0]
    last_ref[...] = hidden_ref[:, height - 1]
    row = local_stats(hidden_ref, length, group_ref[...])
    out_parts_ref[...] = jnp.broadcast_to(row[None], out_parts_ref.shape)


def second_kernel(
    frames_ref, rank_ref, parts_ref, field_ref, above_ref, below_ref, latent_ref, group_ref, gain_ref, shift_ref,
    bias_ref, kernel_hbm,
    keep_ref, send_ref,
    weight_ref, act_ref, acc_ref, sem,
):
    start_weights(kernel_hbm, weight_ref, sem)
    frames, height, columns, channels = field_ref.shape
    clip = lax.axis_index("tm")
    core = lax.rem(clip, 2)
    length = frames_ref[clip]
    start = clip_start_of(frames_ref, rank_ref, clip)
    mean, inverse = combine_stats(parts_ref[:, 0], length, height * columns, group_ref[...])
    activate(field_ref, above_ref, below_ref, act_ref, mean, inverse * gain_ref[...], shift_ref[...])
    convolve(act_ref, weight_ref, sem, kernel_hbm, acc_ref, frames, height)
    pixels = height * columns
    for f in range(frames):
        total = acc_ref[f * pixels : (f + 1) * pixels] + bias_ref[...]
        total = latent_ref[f].astype(F32) + total.reshape(height, columns, channels)
        total = total.astype(BF16)
        place = lax.rem(start + f, 4)
        slot = lax.rem(place, 2)
        stays = place // 2 == core

        @pl.when(stays)
        def _():
            keep_ref[slot] = total

        @pl.when(jnp.logical_not(stays))
        def _():
            send_ref[slot] = total


def spread_kernel(frames_ref, rank_ref, keep_ref, got_ref, out_ref):
    clip = lax.axis_index("tm")
    core = lax.rem(clip, 2)
    other = clip + 1 - 2 * core
    start = clip_start_of(frames_ref, rank_ref, other)
    length = frames_ref[other]
    for chip in range(out_ref.shape[0]):
        for slot in range(2):
            place = 4 * chip + 2 * core + slot - start
            theirs = (place >= 0) & (place < length)
            out_ref[chip, slot] = jnp.where(theirs, got_ref[slot], keep_ref[slot])


def pick_kernel(frames_ref, rank_ref, got_hbm, out_hbm, sem):
    clip = lax.axis_index("tm")
    copies = []
    for slot in range(2):
        place = 2 * clip + slot
        source = jnp.int32(0)
        for k in range(frames_ref.shape[0]):
            offset = place - clip_start_of(frames_ref, rank_ref, k)
            source = source + jnp.where((offset >= 0) & (offset < frames_ref[k]), k // 2, 0)
        copies.append(pltpu.make_async_copy(got_hbm.at[source, slot], out_hbm.at[slot], sem.at[slot]))
    for copy in copies:
        copy.start()
    for copy in copies:
        copy.wait()


def call(kernel, in_specs, outs, scratch=(), out_spec=VMEM):
    return pl.pallas_call(
        kernel,
        in_specs=in_specs,
        out_specs=[out_spec] * len(outs),
        out_shape=[jax.ShapeDtypeStruct(shape, kind) for shape, kind in outs],
        scratch_shapes=list(scratch),
        compiler_params=pltpu.CompilerParams(vmem_limit_bytes=LIMIT),
    )


def local(
    latent,
    clip_frames,
    clip_rank,
    group_of,
    gain_first,
    shift_first,
    conv_first,
    bias_first,
    gain_second,
    shift_second,
    conv_second,
    bias_second,
):
    frames, height, columns, channels = latent.shape
    bands = lax.axis_size("space")
    clips = lax.axis_size("tm")
    row = lambda v: v.reshape(1, channels)
    taps = lambda k: k.reshape(9, 3 * channels, channels)
    group_row = row(group_of)
    edge = ((frames, columns, channels), BF16)
    parts_out = ((bands, 1, LANES), F32)

    def gather(parts):
        return lax.all_to_all(parts, "space", 0, 0, tiled=True)

    def halos(first, last):
        above = lax.ppermute(last, "space", [(i, (i + 1) % bands) for i in range(bands)])
        below = lax.ppermute(first, "space", [((i + 1) % bands, i) for i in range(bands)])
        return above, below

    work = [
        pltpu.VMEM((9, 3 * channels, channels), BF16),
        pltpu.VMEM((frames + 2, height + 2, columns, 3 * channels), BF16),
        pltpu.VMEM((frames * height * columns, channels), F32),
        pltpu.SemaphoreType.DMA((9,)),
    ]

    parts, first, last = call(stats_kernel, [SMEM, VMEM, VMEM], [parts_out, edge, edge])(clip_frames, latent, group_row)
    above, below = halos(first, last)
    parts = gather(parts)
    hidden, parts, first, last = call(
        first_kernel, [SMEM] + [VMEM] * 8 + [HBM], [(latent.shape, BF16), parts_out, edge, edge], work
    )(clip_frames, parts, latent, above, below, group_row, row(gain_first), row(shift_first), row(bias_first), taps(conv_first))
    above, below = halos(first, last)
    parts = gather(parts)
    half = ((2, height, columns, channels), BF16)
    keep, send = call(second_kernel, [SMEM] * 2 + [VMEM] * 9 + [HBM], [half, half], work)(
        clip_frames, clip_rank, parts, hidden, above, below, latent, group_row, row(gain_second), row(shift_second),
        row(bias_second), taps(conv_second),
    )
    got = lax.ppermute(send, "tm", [(i, i ^ 1) for i in range(clips)])
    chips = clips // 2
    (spread,) = call(spread_kernel, [SMEM] * 2 + [VMEM] * 2, [((chips,) + half[0], BF16)])(clip_frames, clip_rank, keep, got)
    groups = [[core + 2 * chip for chip in range(chips)] for core in range(2)]
    spread = lax.all_to_all(spread, "tm", 0, 0, axis_index_groups=groups, tiled=True)
    (out,) = call(pick_kernel, [SMEM] * 2 + [HBM], [half], [pltpu.SemaphoreType.DMA((2,))], HBM)(clip_frames, clip_rank, spread)
    return out


def solution(mesh):
    placed = (P("tm", "space", None, None), P(), P(), P(), P(), P(), P(), P(), P(), P(), P(), P())
    return jax.shard_map(
        local, mesh=mesh, in_specs=placed, out_specs=P("tm", "space", None, None), check_vma=False
    )
```

```python
import functools

import jax
import jax.numpy as jnp
from jax import lax
from jax.experimental import pallas as pl
from jax.experimental.pallas import tpu as pltpu
from jax.sharding import PartitionSpec as P

G = 32
LANES = 128
EPSILON = 1e-06
HIGH = lax.Precision.HIGHEST
F32 = jnp.float32
BF16 = jnp.bfloat16
VMEM = pl.BlockSpec(memory_space=pltpu.VMEM)
SMEM = pl.BlockSpec(memory_space=pltpu.SMEM)
HBM = pl.BlockSpec(memory_space=pltpu.HBM)
LIMIT = 20 * 1024 * 1024


def dot_high(a, b, contract):
    return lax.dot_general(a, b, ((contract[:1], contract[1:]), ((), ())), precision=HIGH, preferred_element_type=F32)


def member_rows(group_row, first):
    channels = group_row.shape[1]
    rows = lax.broadcasted_iota(jnp.int32, (LANES, channels), 0)
    return (rows - first == group_row).astype(F32)


def clip_start_of(frames_ref, rank_ref, clip):
    start = jnp.int32(0)
    for k in range(frames_ref.shape[0]):
        start = start + jnp.where(rank_ref[k] < rank_ref[clip], frames_ref[k], 0)
    return start


def local_stats(field_ref, length, group_row):
    frames, height, columns, channels = field_ref.shape
    pixels = height * columns
    scale = 1.0 / (length.astype(F32) * float(pixels * (channels // G)))
    live = [jnp.where(f < length, 1.0, 0.0).astype(F32) for f in range(frames)]

    def frame(f):
        return field_ref[f].astype(F32).reshape(pixels, channels)

    total = jnp.zeros((1, channels), F32)
    for f in range(frames):
        total = total + live[f] * jnp.sum(frame(f), axis=0, keepdims=True)
    mean_rows = member_rows(group_row, 0)
    group_mean = dot_high(jnp.broadcast_to(total, (8, channels)), mean_rows, (1, 1)) * scale
    mean = dot_high(group_mean, mean_rows, (1, 0))[:1]
    spread = jnp.zeros((1, channels), F32)
    for f in range(frames):
        centred = frame(f) - mean
        spread = spread + live[f] * jnp.sum(centred * centred, axis=0, keepdims=True)
    group_spread = dot_high(jnp.broadcast_to(spread, (8, channels)), member_rows(group_row, G), (1, 1))
    return (group_mean + group_spread)[:1]


def combine_stats(parts, length, pixels, group_row):
    bands = parts.shape[0]
    channels = group_row.shape[1]
    per_band = length.astype(F32) * float(pixels * (channels // G))
    lane = lax.broadcasted_iota(jnp.int32, (1, LANES), 1)
    sums = jnp.sum(parts, axis=0, keepdims=True)
    mean = sums * (1.0 / bands)
    away = parts - mean
    between = jnp.sum(away * away, axis=0, keepdims=True) * per_band
    spread = jnp.where(lane < G, between, jnp.where(lane < 2 * G, sums, 0.0))
    mean = jnp.where(lane < G, mean, 0.0)
    which = lax.broadcasted_iota(jnp.int32, (8, LANES), 0)
    both = jnp.where(which == 0, mean, spread)
    spread_back = dot_high(both, member_rows(group_row, 0) + member_rows(group_row, G), (1, 0))
    variance = spread_back[1:2] / (per_band * bands)
    return spread_back[:1], lax.rsqrt(variance + EPSILON)


def activate(field_ref, above_ref, below_ref, act_ref, mean, scale, shift):
    frames, height, columns, channels = field_ref.shape
    band = lax.axis_index("space")
    top = band == 0
    bottom = band == lax.axis_size("space") - 1
    for f in range(frames):
        for r in range(height + 2):
            if r == 0:
                value = jnp.where(top, field_ref[f, 0], above_ref[f])
            elif r == height + 1:
                value = jnp.where(bottom, field_ref[f, height - 1], below_ref[f])
            else:
                value = field_ref[f, r - 1]
            half = ((value.astype(F32) - mean) * scale + shift) * 0.5
            act = half * jnp.tanh(half) + half
            left = jnp.concatenate([act[:1], act[:-1]], axis=0)
            right = jnp.concatenate([act[1:], act[-1:]], axis=0)
            for step, taken in enumerate((left, act, right)):
                taken = taken.astype(BF16)
                lanes = slice(step * channels, (step + 1) * channels)
                for place in (0, 1, 2) if f == 0 else (f + 2,):
                    act_ref[place, r, :, lanes] = taken


def convolve(act_ref, weight_ref, acc_ref, frames, height):
    columns, width = act_ref.shape[2:]
    rows = frames * height * columns
    for tap in range(9):
        back_step, row_step = divmod(tap, 3)
        slab = act_ref[back_step : back_step + frames, row_step : row_step + height].reshape(rows, width)
        part = jnp.dot(slab, weight_ref[tap], preferred_element_type=F32)
        if tap == 0:
            acc_ref[...] = part
        else:
            acc_ref[...] += part


def in_hbm(array):
    return pltpu.with_memory_space_constraint(array, pltpu.HBM)


def stats_kernel(frames_hbm, rank_hbm, latent_hbm, *rest):
    rows = len(rest) // 2 - 4
    rows_hbm, rest = rest[:rows], rest[rows:]
    parts_ref, first_ref, last_ref, latent_ref, frames_ref, rank_ref = rest[:6]
    rows_ref, (frames_smem, sem) = rest[6 : 6 + rows], rest[6 + rows :]
    group_ref = rows_ref[0]
    pairs = [(frames_hbm, frames_smem), (latent_hbm, latent_ref)]
    pairs += list(zip(rows_hbm, rows_ref)) + [(frames_hbm, frames_ref), (rank_hbm, rank_ref)]
    copies = [pltpu.make_async_copy(source, target, sem.at[i]) for i, (source, target) in enumerate(pairs)]
    for copy in copies:
        copy.start()
    for copy in copies[:3]:
        copy.wait()
    length = frames_smem[lax.axis_index("tm")]
    height = latent_ref.shape[1]
    first_ref[...] = latent_ref[:, 0]
    last_ref[...] = latent_ref[:, height - 1]
    row = local_stats(latent_ref, length, group_ref[...])
    parts_ref[...] = jnp.broadcast_to(row[None], parts_ref.shape)
    for copy in copies[3:]:
        copy.wait()


def first_kernel(
    frames_ref, parts_ref, field_ref, above_ref, below_ref, group_ref, gain_ref, shift_ref, bias_ref, weight_ref,
    hidden_ref, out_parts_ref, first_ref, last_ref,
    act_ref, acc_ref,
):
    frames, height, columns, channels = field_ref.shape
    length = frames_ref[lax.axis_index("tm")]
    mean, inverse = combine_stats(parts_ref[:, 0], length, height * columns, group_ref[...])
    activate(field_ref, above_ref, below_ref, act_ref, mean, inverse * gain_ref[...], shift_ref[...])
    convolve(act_ref, weight_ref, acc_ref, frames, height)
    hidden = (acc_ref[...] + bias_ref[...]).astype(BF16).reshape(hidden_ref.shape)
    hidden_ref[...] = hidden
    first_ref[...] = hidden_ref[:, 0]
    last_ref[...] = hidden_ref[:, height - 1]
    row = local_stats(hidden_ref, length, group_ref[...])
    out_parts_ref[...] = jnp.broadcast_to(row[None], out_parts_ref.shape)


def second_kernel(
    frames_ref, rank_ref, parts_ref, field_ref, above_ref, below_ref, latent_ref, group_ref, gain_ref, shift_ref,
    bias_ref, weight_ref,
    keep_ref, send_ref,
    act_ref, acc_ref,
):
    frames, height, columns, channels = field_ref.shape
    clip = lax.axis_index("tm")
    core = lax.rem(clip, 2)
    length = frames_ref[clip]
    start = clip_start_of(frames_ref, rank_ref, clip)
    mean, inverse = combine_stats(parts_ref[:, 0], length, height * columns, group_ref[...])
    activate(field_ref, above_ref, below_ref, act_ref, mean, inverse * gain_ref[...], shift_ref[...])
    convolve(act_ref, weight_ref, acc_ref, frames, height)
    pixels = height * columns
    for f in range(frames):
        total = acc_ref[f * pixels : (f + 1) * pixels] + bias_ref[...]
        total = latent_ref[f].astype(F32) + total.reshape(height, columns, channels)
        total = total.astype(BF16)
        place = lax.rem(start + f, 4)
        slot = lax.rem(place, 2)
        stays = place // 2 == core

        @pl.when(stays)
        def _():
            keep_ref[slot] = total

        @pl.when(jnp.logical_not(stays))
        def _():
            send_ref[slot] = total


def spread_kernel(frames_ref, rank_ref, keep_ref, got_ref, out_ref):
    clip = lax.axis_index("tm")
    core = lax.rem(clip, 2)
    other = clip + 1 - 2 * core
    start = clip_start_of(frames_ref, rank_ref, other)
    length = frames_ref[other]
    for chip in range(out_ref.shape[0]):
        for slot in range(2):
            place = 4 * chip + 2 * core + slot - start
            theirs = (place >= 0) & (place < length)
            out_ref[chip, slot] = jnp.where(theirs, got_ref[slot], keep_ref[slot])


def pick_kernel(frames_ref, rank_ref, got_hbm, out_hbm, sem):
    clip = lax.axis_index("tm")
    copies = []
    for slot in range(2):
        place = 2 * clip + slot
        source = jnp.int32(0)
        for k in range(frames_ref.shape[0]):
            offset = place - clip_start_of(frames_ref, rank_ref, k)
            source = source + jnp.where((offset >= 0) & (offset < frames_ref[k]), k // 2, 0)
        copies.append(pltpu.make_async_copy(got_hbm.at[source, slot], out_hbm.at[slot], sem.at[slot]))
    for copy in copies:
        copy.start()
    for copy in copies:
        copy.wait()


def call(kernel, in_specs, outs, scratch=(), out_spec=VMEM, cost=None):
    return pl.pallas_call(
        kernel,
        in_specs=in_specs,
        out_specs=[out_spec] * len(outs),
        out_shape=[jax.ShapeDtypeStruct(shape, kind) for shape, kind in outs],
        scratch_shapes=list(scratch),
        compiler_params=pltpu.CompilerParams(vmem_limit_bytes=LIMIT),
        cost_estimate=cost,
    )


def local(
    latent,
    clip_frames,
    clip_rank,
    group_of,
    gain_first,
    shift_first,
    conv_first,
    bias_first,
    gain_second,
    shift_second,
    conv_second,
    bias_second,
):
    frames, height, columns, channels = latent.shape
    bands = lax.axis_size("space")
    clips = lax.axis_size("tm")
    row = lambda v: v.reshape(1, channels)
    taps = lambda k: k.reshape(9, 3 * channels, channels)
    group_row = row(group_of)
    edge = ((frames, columns, channels), BF16)
    parts_out = ((bands, 1, LANES), F32)

    def gather(parts):
        return lax.all_to_all(parts, "space", 0, 0, tiled=True)

    def halos(first, last):
        above = lax.ppermute(last, "space", [(i, (i + 1) % bands) for i in range(bands)])
        below = lax.ppermute(first, "space", [((i + 1) % bands, i) for i in range(bands)])
        return above, below

    work = [
        pltpu.VMEM((frames + 2, height + 2, columns, 3 * channels), BF16),
        pltpu.VMEM((frames * height * columns, channels), F32),
    ]

    vectors = [row(v) for v in (group_of, gain_first, shift_first, bias_first, gain_second, shift_second, bias_second)]
    outs = [parts_out, edge, edge, (latent.shape, BF16), (clip_frames.shape, jnp.int32), (clip_rank.shape, jnp.int32)]
    outs += [(v.shape, v.dtype) for v in vectors]
    parts, first, last, latent, clip_frames, clip_rank, *vectors = call(
        stats_kernel, [HBM] * (3 + len(vectors)), outs,
        [pltpu.SMEM(clip_frames.shape, jnp.int32), pltpu.SemaphoreType.DMA((4 + len(vectors),))],
        cost=pl.CostEstimate(flops=1 << 32, bytes_accessed=1 << 24, transcendentals=0),
    )(*map(in_hbm, (clip_frames, clip_rank, latent, *vectors)))
    group_row = vectors[0]
    above, below = halos(first, last)
    parts = gather(parts)
    hidden, parts, first, last = call(
        first_kernel, [SMEM] + [VMEM] * 9, [(latent.shape, BF16), parts_out, edge, edge], work
    )(clip_frames, parts, latent, above, below, *vectors[:4], taps(conv_first))
    above, below = halos(first, last)
    parts = gather(parts)
    half = ((2, height, columns, channels), BF16)
    keep, send = call(second_kernel, [SMEM] * 2 + [VMEM] * 10, [half, half], work)(
        clip_frames, clip_rank, parts, hidden, above, below, latent, group_row, *vectors[4:], taps(conv_second),
    )
    got = lax.ppermute(send, "tm", [(i, i ^ 1) for i in range(clips)])
    chips = clips // 2
    (spread,) = call(spread_kernel, [SMEM] * 2 + [VMEM] * 2, [((chips,) + half[0], BF16)])(clip_frames, clip_rank, keep, got)
    groups = [[core + 2 * chip for chip in range(chips)] for core in range(2)]
    spread = lax.all_to_all(spread, "tm", 0, 0, axis_index_groups=groups, tiled=True)
    (out,) = call(pick_kernel, [SMEM] * 2 + [pl.BlockSpec(memory_space=pl.ANY)], [half], [pltpu.SemaphoreType.DMA((2,))], HBM)(clip_frames, clip_rank, spread)
    return out


def solution(mesh):
    placed = (P("tm", "space", None, None), P(), P(), P(), P(), P(), P(), P(), P(), P(), P(), P())
    return jax.shard_map(
        local, mesh=mesh, in_specs=placed, out_specs=P("tm", "space", None, None), check_vma=False
    )
```

```python
import functools

import jax
import jax.numpy as jnp
from jax import lax
from jax.experimental import pallas as pl
from jax.experimental.pallas import tpu as pltpu
from jax.sharding import PartitionSpec as P

G = 32
LANES = 128
EPSILON = 1e-06
HIGH = lax.Precision.HIGHEST
F32 = jnp.float32
BF16 = jnp.bfloat16
VMEM = pl.BlockSpec(memory_space=pltpu.VMEM)
SMEM = pl.BlockSpec(memory_space=pltpu.SMEM)
HBM = pl.BlockSpec(memory_space=pltpu.HBM)
LIMIT = 20 * 1024 * 1024


def dot_high(a, b, contract):
    return lax.dot_general(a, b, ((contract[:1], contract[1:]), ((), ())), precision=HIGH, preferred_element_type=F32)


def member_rows(group_row, first):
    channels = group_row.shape[1]
    rows = lax.broadcasted_iota(jnp.int32, (LANES, channels), 0)
    return (rows - first == group_row).astype(F32)


def clip_start_of(frames_ref, rank_ref, clip):
    start = jnp.int32(0)
    for k in range(frames_ref.shape[0]):
        start = start + jnp.where(rank_ref[k] < rank_ref[clip], frames_ref[k], 0)
    return start


def local_stats(field_ref, length, group_row):
    frames, height, columns, channels = field_ref.shape
    pixels = height * columns
    scale = 1.0 / (length.astype(F32) * float(pixels * (channels // G)))
    live = [jnp.where(f < length, 1.0, 0.0).astype(F32) for f in range(frames)]

    def frame(f):
        return field_ref[f].astype(F32).reshape(pixels, channels)

    total = jnp.zeros((1, channels), F32)
    for f in range(frames):
        total = total + live[f] * jnp.sum(frame(f), axis=0, keepdims=True)
    mean_rows = member_rows(group_row, 0)
    group_mean = dot_high(jnp.broadcast_to(total, (8, channels)), mean_rows, (1, 1)) * scale
    mean = dot_high(group_mean, mean_rows, (1, 0))[:1]
    spread = jnp.zeros((1, channels), F32)
    for f in range(frames):
        centred = frame(f) - mean
        spread = spread + live[f] * jnp.sum(centred * centred, axis=0, keepdims=True)
    group_spread = dot_high(jnp.broadcast_to(spread, (8, channels)), member_rows(group_row, G), (1, 1))
    return (group_mean + group_spread)[:1]


def combine_stats(parts, length, pixels, group_row):
    bands = parts.shape[0]
    channels = group_row.shape[1]
    per_band = length.astype(F32) * float(pixels * (channels // G))
    lane = lax.broadcasted_iota(jnp.int32, (1, LANES), 1)
    sums = jnp.sum(parts, axis=0, keepdims=True)
    mean = sums * (1.0 / bands)
    away = parts - mean
    between = jnp.sum(away * away, axis=0, keepdims=True) * per_band
    spread = jnp.where(lane < G, between, jnp.where(lane < 2 * G, sums, 0.0))
    mean = jnp.where(lane < G, mean, 0.0)
    which = lax.broadcasted_iota(jnp.int32, (8, LANES), 0)
    both = jnp.where(which == 0, mean, spread)
    spread_back = dot_high(both, member_rows(group_row, 0) + member_rows(group_row, G), (1, 0))
    variance = spread_back[1:2] / (per_band * bands)
    return spread_back[:1], lax.rsqrt(variance + EPSILON)


def activate(rows, act_ref, mean, scale, shift):
    channels = mean.shape[1]
    for f in range(act_ref.shape[0]):
        for r in range(act_ref.shape[1]):
            half = ((rows(f, r).astype(F32) - mean) * scale + shift) * 0.5
            act = half * jnp.tanh(half) + half
            left = jnp.concatenate([act[:1], act[:-1]], axis=0)
            right = jnp.concatenate([act[1:], act[-1:]], axis=0)
            for step, taken in enumerate((left, act, right)):
                act_ref[f, r, :, step * channels : (step + 1) * channels] = taken.astype(BF16)


def convolve(act_ref, weight_ref, acc_refs):
    frames, height, columns, width = act_ref.shape
    height = height - 2
    for back_step, acc_ref in enumerate(acc_refs):
        used = frames - 2 + back_step
        slabs = [act_ref[:used, j : j + height].reshape(used * height * columns, width) for j in range(3)]
        kernel = weight_ref[3 * back_step : 3 * back_step + 3].reshape(3 * width, -1)
        part = jnp.dot(jnp.concatenate(slabs, axis=1), kernel, preferred_element_type=F32)
        acc_ref[...] = part.reshape(acc_ref.shape)


def frame_sum(acc_refs, f, zero):
    return acc_refs[0][max(f - 2, 0) + zero] + acc_refs[1][max(f - 1, 0) + zero] + acc_refs[2][f + zero]


def band_ends():
    band = lax.axis_index("space")
    return band == 0, band == lax.axis_size("space") - 1


def in_hbm(array):
    return pltpu.with_memory_space_constraint(array, pltpu.HBM)


def stats_kernel(frames_hbm, rank_hbm, latent_hbm, *rest):
    rows = len(rest) // 2 - 3
    rows_hbm, rest = rest[:rows], rest[rows:]
    parts_ref, latent_ref, frames_ref, rank_ref = rest[:4]
    rows_ref, (frames_smem, sem) = rest[4 : 4 + rows], rest[4 + rows :]
    group_ref = rows_ref[0]
    pairs = [(frames_hbm, frames_smem), (latent_hbm, latent_ref)]
    pairs += list(zip(rows_hbm, rows_ref)) + [(frames_hbm, frames_ref), (rank_hbm, rank_ref)]
    copies = [pltpu.make_async_copy(source, target, sem.at[i]) for i, (source, target) in enumerate(pairs)]
    for copy in copies:
        copy.start()
    for copy in copies[:3]:
        copy.wait()
    length = frames_smem[lax.axis_index("tm")]
    row = local_stats(latent_ref, length, group_ref[...])
    parts_ref[...] = jnp.broadcast_to(row[None], parts_ref.shape)
    for copy in copies[3:]:
        copy.wait()


def first_kernel(
    frames_ref, parts_ref, field_ref, above_ref, below_ref, group_ref, gain_ref, shift_ref, bias_ref, weight_ref,
    hidden_ref, out_parts_ref,
    own_ref, act_ref, *acc_refs,
):
    frames, height, columns, channels = field_ref.shape
    length = frames_ref[lax.axis_index("tm")]
    zero = jnp.minimum(length, 0)
    top, bottom = band_ends()
    mean, inverse = combine_stats(parts_ref[:, 0], length, height * columns, group_ref[...])

    def rows(f, r):
        if r < 2:
            row = above_ref[f, height - 2 + r]
            return jnp.where(top, field_ref[f, 0], row) if r == 1 else row
        if r >= height + 2:
            row = below_ref[f, r - height - 2]
            return jnp.where(bottom, field_ref[f, height - 1], row) if r == height + 2 else row
        return field_ref[f, r - 2]

    activate(rows, act_ref, mean, inverse * gain_ref[...], shift_ref[...])
    convolve(act_ref, weight_ref, acc_refs)
    for f in range(frames):
        hidden = (frame_sum(acc_refs, f, zero) + bias_ref[...]).astype(BF16)
        hidden_ref[f] = hidden
        own_ref[f] = hidden[1 : height + 1]
    row = local_stats(own_ref, length, group_ref[...])
    out_parts_ref[...] = jnp.broadcast_to(row[None], out_parts_ref.shape)


def second_kernel(
    frames_ref, rank_ref, parts_ref, hidden_ref, latent_ref, group_ref, gain_ref, shift_ref, bias_ref, weight_ref,
    keep_ref, send_ref,
    act_ref, *acc_refs,
):
    frames, height, columns, channels = latent_ref.shape
    clip = lax.axis_index("tm")
    core = lax.rem(clip, 2)
    length = frames_ref[clip]
    zero = jnp.minimum(length, 0)
    start = clip_start_of(frames_ref, rank_ref, clip)
    top, bottom = band_ends()
    mean, inverse = combine_stats(parts_ref[:, 0], length, height * columns, group_ref[...])

    def rows(f, r):
        row = hidden_ref[f, r]
        if r == 0:
            return jnp.where(top, hidden_ref[f, 1], row)
        return jnp.where(bottom, hidden_ref[f, height], row) if r == height + 1 else row

    activate(rows, act_ref, mean, inverse * gain_ref[...], shift_ref[...])
    convolve(act_ref, weight_ref, acc_refs)
    for f in range(frames):
        total = (latent_ref[f].astype(F32) + (frame_sum(acc_refs, f, zero) + bias_ref[...])).astype(BF16)
        place = lax.rem(start + f, 4)
        slot = lax.rem(place, 2)
        stays = place // 2 == core

        @pl.when(stays)
        def _():
            keep_ref[slot] = total

        @pl.when(jnp.logical_not(stays))
        def _():
            send_ref[slot] = total


def spread_kernel(frames_ref, rank_ref, keep_ref, got_ref, out_ref):
    clip = lax.axis_index("tm")
    core = lax.rem(clip, 2)
    other = clip + 1 - 2 * core
    start = clip_start_of(frames_ref, rank_ref, other)
    length = frames_ref[other]
    for chip in range(out_ref.shape[0]):
        for slot in range(2):
            place = 4 * chip + 2 * core + slot - start
            theirs = (place >= 0) & (place < length)
            out_ref[chip, slot] = jnp.where(theirs, got_ref[slot], keep_ref[slot])


def pick_kernel(frames_ref, rank_ref, got_hbm, out_hbm, sem):
    clip = lax.axis_index("tm")
    copies = []
    for slot in range(2):
        place = 2 * clip + slot
        source = jnp.int32(0)
        for k in range(frames_ref.shape[0]):
            offset = place - clip_start_of(frames_ref, rank_ref, k)
            source = source + jnp.where((offset >= 0) & (offset < frames_ref[k]), k // 2, 0)
        copies.append(pltpu.make_async_copy(got_hbm.at[source, slot], out_hbm.at[slot], sem.at[slot]))
    for copy in copies:
        copy.start()
    for copy in copies:
        copy.wait()


def call(kernel, in_specs, outs, scratch=(), out_spec=VMEM, cost=None):
    return pl.pallas_call(
        kernel,
        in_specs=in_specs,
        out_specs=[out_spec] * len(outs),
        out_shape=[jax.ShapeDtypeStruct(shape, kind) for shape, kind in outs],
        scratch_shapes=list(scratch),
        compiler_params=pltpu.CompilerParams(vmem_limit_bytes=LIMIT),
        cost_estimate=cost,
    )


def local(
    latent,
    clip_frames,
    clip_rank,
    group_of,
    gain_first,
    shift_first,
    conv_first,
    bias_first,
    gain_second,
    shift_second,
    conv_second,
    bias_second,
):
    frames, height, columns, channels = latent.shape
    bands = lax.axis_size("space")
    clips = lax.axis_size("tm")
    row = lambda v: v.reshape(1, channels)
    taps = lambda k: k.reshape(9, 3 * channels, channels)
    group_row = row(group_of)
    parts_out = ((bands, 1, LANES), F32)

    def gather(parts):
        return lax.all_to_all(parts, "space", 0, 0, tiled=True)

    def work(height):
        accs = [pltpu.VMEM((frames - 2 + i, height, columns, channels), F32) for i in range(3)]
        return [pltpu.VMEM((frames, height + 2, columns, 3 * channels), BF16)] + accs

    vectors = [row(v) for v in (group_of, gain_first, shift_first, bias_first, gain_second, shift_second, bias_second)]
    outs = [parts_out, (latent.shape, BF16), (clip_frames.shape, jnp.int32), (clip_rank.shape, jnp.int32)]
    outs += [(v.shape, v.dtype) for v in vectors]
    parts, latent, clip_frames, clip_rank, *vectors = call(
        stats_kernel, [HBM] * (3 + len(vectors)), outs,
        [pltpu.SMEM(clip_frames.shape, jnp.int32), pltpu.SemaphoreType.DMA((4 + len(vectors),))],
        cost=pl.CostEstimate(flops=1 << 32, bytes_accessed=1 << 24, transcendentals=0),
    )(*map(in_hbm, (clip_frames, clip_rank, latent, *vectors)))
    group_row = vectors[0]
    above = lax.ppermute(latent, "space", [(i, (i + 1) % bands) for i in range(bands)])
    below = lax.ppermute(latent, "space", [((i + 1) % bands, i) for i in range(bands)])
    parts = gather(parts)
    hidden, parts = call(
        first_kernel, [SMEM] + [VMEM] * 9,
        [((frames, height + 2, columns, channels), BF16), parts_out],
        [pltpu.VMEM(latent.shape, BF16)] + work(height + 2),
    )(clip_frames, parts, latent, above, below, *vectors[:4], taps(conv_first))
    parts = gather(parts)
    half = ((2, height, columns, channels), BF16)
    keep, send = call(second_kernel, [SMEM] * 2 + [VMEM] * 8, [half, half], work(height))(
        clip_frames, clip_rank, parts, hidden, latent, group_row, *vectors[4:], taps(conv_second),
    )
    got = lax.ppermute(send, "tm", [(i, i ^ 1) for i in range(clips)])
    chips = clips // 2
    (spread,) = call(spread_kernel, [SMEM] * 2 + [VMEM] * 2, [((chips,) + half[0], BF16)])(clip_frames, clip_rank, keep, got)
    groups = [[core + 2 * chip for chip in range(chips)] for core in range(2)]
    spread = lax.all_to_all(spread, "tm", 0, 0, axis_index_groups=groups, tiled=True)
    (out,) = call(pick_kernel, [SMEM] * 2 + [pl.BlockSpec(memory_space=pl.ANY)], [half], [pltpu.SemaphoreType.DMA((2,))], HBM)(clip_frames, clip_rank, spread)
    return out


def solution(mesh):
    placed = (P("tm", "space", None, None), P(), P(), P(), P(), P(), P(), P(), P(), P(), P(), P())
    return jax.shard_map(
        local, mesh=mesh, in_specs=placed, out_specs=P("tm", "space", None, None), check_vma=False
    )
```

```python
import functools

import jax
import jax.numpy as jnp
from jax import lax
from jax.experimental import pallas as pl
from jax.experimental.pallas import tpu as pltpu
from jax.sharding import PartitionSpec as P

G = 32
LANES = 128
EPSILON = 1e-06
HIGH = lax.Precision.HIGHEST
F32 = jnp.float32
BF16 = jnp.bfloat16
VMEM = pl.BlockSpec(memory_space=pltpu.VMEM)
SMEM = pl.BlockSpec(memory_space=pltpu.SMEM)
HBM = pl.BlockSpec(memory_space=pltpu.HBM)
LIMIT = 20 * 1024 * 1024


def dot_high(a, b, contract):
    return lax.dot_general(a, b, ((contract[:1], contract[1:]), ((), ())), precision=HIGH, preferred_element_type=F32)


def member_rows(group_row, first):
    channels = group_row.shape[1]
    rows = lax.broadcasted_iota(jnp.int32, (LANES, channels), 0)
    return (rows - first == group_row).astype(F32)


def clip_start_of(frames_ref, rank_ref, clip):
    start = jnp.int32(0)
    for k in range(frames_ref.shape[0]):
        start = start + jnp.where(rank_ref[k] < rank_ref[clip], frames_ref[k], 0)
    return start


def local_stats(field_ref, length, group_row):
    frames, height, columns, channels = field_ref.shape
    pixels = height * columns
    scale = 1.0 / (length.astype(F32) * float(pixels * (channels // G)))
    live = [jnp.where(f < length, 1.0, 0.0).astype(F32) for f in range(frames)]

    def frame(f):
        return field_ref[f].astype(F32).reshape(pixels, channels)

    total = jnp.zeros((1, channels), F32)
    for f in range(frames):
        total = total + live[f] * jnp.sum(frame(f), axis=0, keepdims=True)
    mean_rows = member_rows(group_row, 0)
    group_mean = dot_high(jnp.broadcast_to(total, (8, channels)), mean_rows, (1, 1)) * scale
    mean = dot_high(group_mean, mean_rows, (1, 0))[:1]
    spread = jnp.zeros((1, channels), F32)
    for f in range(frames):
        centred = frame(f) - mean
        spread = spread + live[f] * jnp.sum(centred * centred, axis=0, keepdims=True)
    group_spread = dot_high(jnp.broadcast_to(spread, (8, channels)), member_rows(group_row, G), (1, 1))
    return (group_mean + group_spread)[:1]


def combine_stats(parts, length, pixels, group_row):
    bands = parts.shape[0]
    channels = group_row.shape[1]
    per_band = length.astype(F32) * float(pixels * (channels // G))
    lane = lax.broadcasted_iota(jnp.int32, (1, LANES), 1)
    sums = jnp.sum(parts, axis=0, keepdims=True)
    mean = sums * (1.0 / bands)
    away = parts - mean
    between = jnp.sum(away * away, axis=0, keepdims=True) * per_band
    spread = jnp.where(lane < G, between, jnp.where(lane < 2 * G, sums, 0.0))
    mean = jnp.where(lane < G, mean, 0.0)
    which = lax.broadcasted_iota(jnp.int32, (8, LANES), 0)
    both = jnp.where(which == 0, mean, spread)
    spread_back = dot_high(both, member_rows(group_row, 0) + member_rows(group_row, G), (1, 0))
    variance = spread_back[1:2] / (per_band * bands)
    return spread_back[:1], lax.rsqrt(variance + EPSILON)


def activate(rows, act_ref, mean, scale, shift):
    channels = mean.shape[1]
    for f in range(act_ref.shape[0]):
        for r in range(act_ref.shape[1]):
            half = ((rows(f, r).astype(F32) - mean) * scale + shift) * 0.5
            act = half * jnp.tanh(half) + half
            left = jnp.concatenate([act[:1], act[:-1]], axis=0)
            right = jnp.concatenate([act[1:], act[-1:]], axis=0)
            for step, taken in enumerate((left, act, right)):
                act_ref[f, r, :, step * channels : (step + 1) * channels] = taken.astype(BF16)


def convolve(act_ref, weight_ref, acc_refs):
    frames, height, columns, width = act_ref.shape
    height = height - 2
    for back_step, acc_ref in enumerate(acc_refs):
        used = frames - 2 + back_step
        slabs = [act_ref[:used, j : j + height].reshape(used * height * columns, width) for j in range(3)]
        kernel = weight_ref[3 * back_step : 3 * back_step + 3].reshape(3 * width, -1)
        part = jnp.dot(jnp.concatenate(slabs, axis=1), kernel, preferred_element_type=F32)
        acc_ref[...] = part.reshape(acc_ref.shape)


def frame_sum(acc_refs, f, zero):
    return acc_refs[0][max(f - 2, 0) + zero] + acc_refs[1][max(f - 1, 0) + zero] + acc_refs[2][f + zero]


def band_ends():
    band = lax.axis_index("space")
    return band == 0, band == lax.axis_size("space") - 1


def in_hbm(array):
    return pltpu.with_memory_space_constraint(array, pltpu.HBM)


def stats_kernel(frames_hbm, rank_hbm, latent_hbm, *rest):
    rows = len(rest) // 2 - 3
    rows_hbm, rest = rest[:rows], rest[rows:]
    parts_ref, latent_ref, frames_ref, rank_ref = rest[:4]
    rows_ref, (frames_smem, sem) = rest[4 : 4 + rows], rest[4 + rows :]
    group_ref = rows_ref[0]
    pairs = [(frames_hbm, frames_smem), (latent_hbm, latent_ref)]
    pairs += list(zip(rows_hbm, rows_ref)) + [(frames_hbm, frames_ref), (rank_hbm, rank_ref)]
    copies = [pltpu.make_async_copy(source, target, sem.at[i]) for i, (source, target) in enumerate(pairs)]
    for copy in copies:
        copy.start()
    for copy in copies[:3]:
        copy.wait()
    length = frames_smem[lax.axis_index("tm")]
    row = local_stats(latent_ref, length, group_ref[...])
    parts_ref[...] = jnp.broadcast_to(row[None], parts_ref.shape)
    for copy in copies[3:]:
        copy.wait()


def first_kernel(
    frames_ref, parts_ref, field_ref, above_ref, below_ref, group_ref, gain_ref, shift_ref, bias_ref, weight_ref,
    hidden_ref, out_parts_ref,
    own_ref, act_ref, *acc_refs,
):
    frames, height, columns, channels = field_ref.shape
    length = frames_ref[lax.axis_index("tm")]
    zero = jnp.minimum(length, 0)
    top, bottom = band_ends()
    mean, inverse = combine_stats(parts_ref[:, 0], length, height * columns, group_ref[...])

    def rows(f, r):
        if r < 2:
            row = above_ref[f, height - 2 + r]
            return jnp.where(top, field_ref[f, 0], row) if r == 1 else row
        if r >= height + 2:
            row = below_ref[f, r - height - 2]
            return jnp.where(bottom, field_ref[f, height - 1], row) if r == height + 2 else row
        return field_ref[f, r - 2]

    activate(rows, act_ref, mean, inverse * gain_ref[...], shift_ref[...])
    convolve(act_ref, weight_ref, acc_refs)
    for f in range(frames):
        hidden = (frame_sum(acc_refs, f, zero) + bias_ref[...]).astype(BF16)
        hidden_ref[f] = hidden
        own_ref[f] = hidden[1 : height + 1]
    row = local_stats(own_ref, length, group_ref[...])
    out_parts_ref[...] = jnp.broadcast_to(row[None], out_parts_ref.shape)


def second_kernel(
    frames_ref, rank_ref, parts_ref, hidden_ref, latent_ref, group_ref, gain_ref, shift_ref, bias_ref, weight_ref,
    keep_ref, send_ref,
    act_ref, *acc_refs,
):
    frames, height, columns, channels = latent_ref.shape
    clip = lax.axis_index("tm")
    core = lax.rem(clip, 2)
    length = frames_ref[clip]
    zero = jnp.minimum(length, 0)
    start = clip_start_of(frames_ref, rank_ref, clip)
    top, bottom = band_ends()
    mean, inverse = combine_stats(parts_ref[:, 0], length, height * columns, group_ref[...])

    def rows(f, r):
        row = hidden_ref[f, r]
        if r == 0:
            return jnp.where(top, hidden_ref[f, 1], row)
        return jnp.where(bottom, hidden_ref[f, height], row) if r == height + 1 else row

    activate(rows, act_ref, mean, inverse * gain_ref[...], shift_ref[...])
    convolve(act_ref, weight_ref, acc_refs)
    for f in range(frames):
        total = (latent_ref[f].astype(F32) + (frame_sum(acc_refs, f, zero) + bias_ref[...])).astype(BF16)
        place = lax.rem(start + f, 4)
        slot = lax.rem(place, 2)
        stays = place // 2 == core

        @pl.when(stays)
        def _():
            keep_ref[slot] = total

        @pl.when(jnp.logical_not(stays))
        def _():
            send_ref[slot] = total


def spread_kernel(frames_ref, rank_ref, keep_ref, got_ref, out_ref):
    clip = lax.axis_index("tm")
    core = lax.rem(clip, 2)
    other = clip + 1 - 2 * core
    start = clip_start_of(frames_ref, rank_ref, other)
    length = frames_ref[other]
    for chip in range(out_ref.shape[0]):
        for slot in range(2):
            place = 4 * chip + 2 * core + slot - start
            theirs = (place >= 0) & (place < length)
            out_ref[chip, slot] = jnp.where(theirs, got_ref[slot], keep_ref[slot])


def pick_kernel(frames_ref, rank_ref, got_hbm, out_hbm, sem):
    clip = lax.axis_index("tm")
    copies = []
    for slot in range(2):
        place = 2 * clip + slot
        source = jnp.int32(0)
        for k in range(frames_ref.shape[0]):
            offset = place - clip_start_of(frames_ref, rank_ref, k)
            source = source + jnp.where((offset >= 0) & (offset < frames_ref[k]), k // 2, 0)
        copies.append(pltpu.make_async_copy(got_hbm.at[source, slot], out_hbm.at[slot], sem.at[slot]))
    for copy in copies:
        copy.start()
    for copy in copies:
        copy.wait()


def call(kernel, in_specs, outs, scratch=(), out_spec=VMEM, cost=None):
    return pl.pallas_call(
        kernel,
        in_specs=in_specs,
        out_specs=[out_spec] * len(outs),
        out_shape=[jax.ShapeDtypeStruct(shape, kind) for shape, kind in outs],
        scratch_shapes=list(scratch),
        compiler_params=pltpu.CompilerParams(vmem_limit_bytes=LIMIT),
        cost_estimate=cost,
    )


def local(
    latent,
    clip_frames,
    clip_rank,
    group_of,
    gain_first,
    shift_first,
    conv_first,
    bias_first,
    gain_second,
    shift_second,
    conv_second,
    bias_second,
):
    frames, height, columns, channels = latent.shape
    bands = lax.axis_size("space")
    clips = lax.axis_size("tm")
    row = lambda v: v.reshape(1, channels)
    taps = lambda k: k.reshape(9, 3 * channels, channels)
    group_row = row(group_of)
    parts_out = ((bands, 1, LANES), F32)

    def gather(parts):
        return lax.all_to_all(parts, "space", 0, 0, tiled=True)

    def work(height):
        accs = [pltpu.VMEM((frames - 2 + i, height, columns, channels), F32) for i in range(3)]
        return [pltpu.VMEM((frames, height + 2, columns, 3 * channels), BF16)] + accs

    above = lax.ppermute(latent, "space", [(i, (i + 1) % bands) for i in range(bands)])
    below = lax.ppermute(latent, "space", [((i + 1) % bands, i) for i in range(bands)])
    vectors = [row(v) for v in (group_of, gain_first, shift_first, bias_first, gain_second, shift_second, bias_second)]
    outs = [parts_out, (latent.shape, BF16), (clip_frames.shape, jnp.int32), (clip_rank.shape, jnp.int32)]
    outs += [(v.shape, v.dtype) for v in vectors]
    parts, latent, clip_frames, clip_rank, *vectors = call(
        stats_kernel, [HBM] * (3 + len(vectors)), outs,
        [pltpu.SMEM(clip_frames.shape, jnp.int32), pltpu.SemaphoreType.DMA((4 + len(vectors),))],
        cost=pl.CostEstimate(flops=1 << 32, bytes_accessed=1 << 24, transcendentals=0),
    )(*map(in_hbm, (clip_frames, clip_rank, latent, *vectors)))
    group_row = vectors[0]
    parts = gather(parts)
    hidden, parts = call(
        first_kernel, [SMEM] + [VMEM] * 9,
        [((frames, height + 2, columns, channels), BF16), parts_out],
        [pltpu.VMEM(latent.shape, BF16)] + work(height + 2),
    )(clip_frames, parts, latent, above, below, *vectors[:4], taps(conv_first))
    parts = gather(parts)
    half = ((2, height, columns, channels), BF16)
    keep, send = call(second_kernel, [SMEM] * 2 + [VMEM] * 8, [half, half], work(height))(
        clip_frames, clip_rank, parts, hidden, latent, group_row, *vectors[4:], taps(conv_second),
    )
    got = lax.ppermute(send, "tm", [(i, i ^ 1) for i in range(clips)])
    chips = clips // 2
    (spread,) = call(spread_kernel, [SMEM] * 2 + [VMEM] * 2, [((chips,) + half[0], BF16)])(clip_frames, clip_rank, keep, got)
    groups = [[core + 2 * chip for chip in range(chips)] for core in range(2)]
    spread = lax.all_to_all(spread, "tm", 0, 0, axis_index_groups=groups, tiled=True)
    (out,) = call(pick_kernel, [SMEM] * 2 + [pl.BlockSpec(memory_space=pl.ANY)], [half], [pltpu.SemaphoreType.DMA((2,))], HBM)(clip_frames, clip_rank, spread)
    return out


def solution(mesh):
    placed = (P("tm", "space", None, None), P(), P(), P(), P(), P(), P(), P(), P(), P(), P(), P())
    return jax.shard_map(
        local, mesh=mesh, in_specs=placed, out_specs=P("tm", "space", None, None), check_vma=False
    )
```

```python
import functools

import jax
import jax.numpy as jnp
from jax import lax
from jax.experimental import pallas as pl
from jax.experimental.pallas import tpu as pltpu
from jax.sharding import PartitionSpec as P

G = 32
LANES = 128
EPSILON = 1e-06
HIGH = lax.Precision.HIGHEST
F32 = jnp.float32
BF16 = jnp.bfloat16
VMEM = pl.BlockSpec(memory_space=pltpu.VMEM)
SMEM = pl.BlockSpec(memory_space=pltpu.SMEM)
HBM = pl.BlockSpec(memory_space=pltpu.HBM)
ANY = pl.BlockSpec(memory_space=pl.ANY)
LIMIT = 20 * 1024 * 1024


def dot_high(a, b, contract):
    return lax.dot_general(a, b, ((contract[:1], contract[1:]), ((), ())), precision=HIGH, preferred_element_type=F32)


def member_rows(group_row, first):
    channels = group_row.shape[1]
    rows = lax.broadcasted_iota(jnp.int32, (LANES, channels), 0)
    return (rows - first == group_row).astype(F32)


def clip_start_of(frames_ref, rank_ref, clip):
    start = jnp.int32(0)
    for k in range(frames_ref.shape[0]):
        start = start + jnp.where(rank_ref[k] < rank_ref[clip], frames_ref[k], 0)
    return start


def local_stats(field_ref, length, group_row):
    frames, height, columns, channels = field_ref.shape
    pixels = height * columns
    scale = 1.0 / (length.astype(F32) * float(pixels * (channels // G)))
    live = [jnp.where(f < length, 1.0, 0.0).astype(F32) for f in range(frames)]

    def frame(f):
        return field_ref[f].astype(F32).reshape(pixels, channels)

    total = jnp.zeros((1, channels), F32)
    for f in range(frames):
        total = total + live[f] * jnp.sum(frame(f), axis=0, keepdims=True)
    mean_rows = member_rows(group_row, 0)
    group_mean = dot_high(jnp.broadcast_to(total, (8, channels)), mean_rows, (1, 1)) * scale
    mean = dot_high(group_mean, mean_rows, (1, 0))[:1]
    spread = jnp.zeros((1, channels), F32)
    for f in range(frames):
        centred = frame(f) - mean
        spread = spread + live[f] * jnp.sum(centred * centred, axis=0, keepdims=True)
    group_spread = dot_high(jnp.broadcast_to(spread, (8, channels)), member_rows(group_row, G), (1, 1))
    return (group_mean + group_spread)[:1]


def combine_stats(parts, length, pixels, group_row):
    bands = parts.shape[0]
    channels = group_row.shape[1]
    per_band = length.astype(F32) * float(pixels * (channels // G))
    lane = lax.broadcasted_iota(jnp.int32, (1, LANES), 1)
    sums = jnp.sum(parts, axis=0, keepdims=True)
    mean = sums * (1.0 / bands)
    away = parts - mean
    between = jnp.sum(away * away, axis=0, keepdims=True) * per_band
    spread = jnp.where(lane < G, between, jnp.where(lane < 2 * G, sums, 0.0))
    mean = jnp.where(lane < G, mean, 0.0)
    which = lax.broadcasted_iota(jnp.int32, (8, LANES), 0)
    both = jnp.where(which == 0, mean, spread)
    spread_back = dot_high(both, member_rows(group_row, 0) + member_rows(group_row, G), (1, 0))
    variance = spread_back[1:2] / (per_band * bands)
    return spread_back[:1], lax.rsqrt(variance + EPSILON)


def activate(rows, act_ref, mean, scale, shift):
    channels = mean.shape[1]
    for f in range(act_ref.shape[0]):
        for r in range(act_ref.shape[1]):
            half = ((rows(f, r).astype(F32) - mean) * scale + shift) * 0.5
            act = half * jnp.tanh(half) + half
            left = jnp.concatenate([act[:1], act[:-1]], axis=0)
            right = jnp.concatenate([act[1:], act[-1:]], axis=0)
            for step, taken in enumerate((left, act, right)):
                act_ref[f, r, :, step * channels : (step + 1) * channels] = taken.astype(BF16)


def convolve(act_ref, weight_ref, acc_refs):
    frames, height, columns, width = act_ref.shape
    height = height - 2
    for back_step, acc_ref in enumerate(acc_refs):
        used = frames - 2 + back_step
        slabs = [act_ref[:used, j : j + height].reshape(used * height * columns, width) for j in range(3)]
        kernel = weight_ref[3 * back_step : 3 * back_step + 3].reshape(3 * width, -1)
        part = jnp.dot(jnp.concatenate(slabs, axis=1), kernel, preferred_element_type=F32)
        acc_ref[...] = part.reshape(acc_ref.shape)


def frame_sum(acc_refs, f, zero):
    return acc_refs[0][max(f - 2, 0) + zero] + acc_refs[1][max(f - 1, 0) + zero] + acc_refs[2][f + zero]


def band_ends():
    band = lax.axis_index("space")
    return band == 0, band == lax.axis_size("space") - 1


def in_hbm(array):
    return pltpu.with_memory_space_constraint(array, pltpu.HBM)


def stats_kernel(frames_hbm, rank_hbm, latent_hbm, *rest):
    rows = len(rest) // 2 - 3
    rows_hbm, rest = rest[:rows], rest[rows:]
    parts_ref, latent_ref, frames_ref, rank_ref = rest[:4]
    rows_ref, (frames_smem, sem) = rest[4 : 4 + rows], rest[4 + rows :]
    group_ref = rows_ref[0]
    pairs = [(frames_hbm, frames_smem), (latent_hbm, latent_ref)]
    pairs += list(zip(rows_hbm, rows_ref)) + [(frames_hbm, frames_ref), (rank_hbm, rank_ref)]
    copies = [pltpu.make_async_copy(source, target, sem.at[i]) for i, (source, target) in enumerate(pairs)]
    for copy in copies:
        copy.start()
    for copy in copies[:3]:
        copy.wait()
    length = frames_smem[lax.axis_index("tm")]
    row = local_stats(latent_ref, length, group_ref[...])
    parts_ref[...] = jnp.broadcast_to(row[None], parts_ref.shape)
    for copy in copies[3:]:
        copy.wait()


def first_kernel(
    frames_ref, parts_ref, field_ref, above_ref, below_ref, group_ref, gain_ref, shift_ref, bias_ref, weight_ref,
    hidden_ref, out_parts_ref,
    own_ref, act_ref, *acc_refs,
):
    frames, height, columns, channels = field_ref.shape
    length = frames_ref[lax.axis_index("tm")]
    zero = jnp.minimum(length, 0)
    top, bottom = band_ends()
    mean, inverse = combine_stats(parts_ref[:, 0], length, height * columns, group_ref[...])

    def rows(f, r):
        if r < 2:
            row = above_ref[f, height - 2 + r]
            return jnp.where(top, field_ref[f, 0], row) if r == 1 else row
        if r >= height + 2:
            row = below_ref[f, r - height - 2]
            return jnp.where(bottom, field_ref[f, height - 1], row) if r == height + 2 else row
        return field_ref[f, r - 2]

    activate(rows, act_ref, mean, inverse * gain_ref[...], shift_ref[...])
    convolve(act_ref, weight_ref, acc_refs)
    for f in range(frames):
        hidden = (frame_sum(acc_refs, f, zero) + bias_ref[...]).astype(BF16)
        hidden_ref[f] = hidden
        own_ref[f] = hidden[1 : height + 1]
    row = local_stats(own_ref, length, group_ref[...])
    out_parts_ref[...] = jnp.broadcast_to(row[None], out_parts_ref.shape)


def second_kernel(
    frames_ref, rank_ref, parts_ref, hidden_ref, latent_ref, group_ref, gain_ref, shift_ref, bias_ref, weight_ref,
    keep_ref, send_ref,
    act_ref, *acc_refs,
):
    frames, height, columns, channels = latent_ref.shape
    clip = lax.axis_index("tm")
    core = lax.rem(clip, 2)
    length = frames_ref[clip]
    zero = jnp.minimum(length, 0)
    start = clip_start_of(frames_ref, rank_ref, clip)
    top, bottom = band_ends()
    mean, inverse = combine_stats(parts_ref[:, 0], length, height * columns, group_ref[...])

    def rows(f, r):
        row = hidden_ref[f, r]
        if r == 0:
            return jnp.where(top, hidden_ref[f, 1], row)
        return jnp.where(bottom, hidden_ref[f, height], row) if r == height + 1 else row

    activate(rows, act_ref, mean, inverse * gain_ref[...], shift_ref[...])
    convolve(act_ref, weight_ref, acc_refs)
    for f in range(frames):
        total = (latent_ref[f].astype(F32) + (frame_sum(acc_refs, f, zero) + bias_ref[...])).astype(BF16)
        place = lax.rem(start + f, 4)
        slot = lax.rem(place, 2)
        stays = place // 2 == core

        @pl.when(stays)
        def _():
            keep_ref[slot] = total

        @pl.when(jnp.logical_not(stays))
        def _():
            send_ref[slot] = total


def spread_kernel(frames_ref, rank_ref, keep_ref, got_ref, *out_refs):
    clip = lax.axis_index("tm")
    core = lax.rem(clip, 2)
    chips = len(out_refs)
    other = clip + 1 - 2 * core
    start = clip_start_of(frames_ref, rank_ref, other)
    length = frames_ref[other]
    for step, out_ref in enumerate(out_refs):
        chip = lax.rem(clip // 2 + step, chips)
        for slot in range(2):
            place = 4 * chip + 2 * core + slot - start
            theirs = (place >= 0) & (place < length)
            out_ref[slot] = jnp.where(theirs, got_ref[slot], keep_ref[slot])


def pick_kernel(frames_ref, rank_ref, *rest):
    *got_refs, out_hbm, sem = rest
    clip = lax.axis_index("tm")
    chips = len(got_refs)
    starts = [clip_start_of(frames_ref, rank_ref, k) for k in range(frames_ref.shape[0])]
    copies = []
    for slot in range(2):
        place = 2 * clip + slot
        source = jnp.int32(0)
        for k, start in enumerate(starts):
            source = source + jnp.where((place >= start) & (place < start + frames_ref[k]), k // 2, 0)
        step = lax.rem(clip // 2 - source + chips, chips)
        for k, got_ref in enumerate(got_refs):
            copy = pltpu.make_async_copy(got_ref.at[slot], out_hbm.at[slot], sem.at[slot])
            pl.when(step == k)(copy.start)
        copies.append(copy)
    for copy in copies:
        copy.wait()


def call(kernel, in_specs, outs, scratch=(), out_spec=VMEM, cost=None):
    return pl.pallas_call(
        kernel,
        in_specs=in_specs,
        out_specs=[out_spec] * len(outs),
        out_shape=[jax.ShapeDtypeStruct(shape, kind) for shape, kind in outs],
        scratch_shapes=list(scratch),
        compiler_params=pltpu.CompilerParams(vmem_limit_bytes=LIMIT),
        cost_estimate=cost,
    )


def local(
    latent,
    clip_frames,
    clip_rank,
    group_of,
    gain_first,
    shift_first,
    conv_first,
    bias_first,
    gain_second,
    shift_second,
    conv_second,
    bias_second,
):
    frames, height, columns, channels = latent.shape
    bands = lax.axis_size("space")
    clips = lax.axis_size("tm")
    row = lambda v: v.reshape(1, channels)
    taps = lambda k: k.reshape(9, 3 * channels, channels)
    group_row = row(group_of)
    parts_out = ((bands, 1, LANES), F32)

    def gather(parts):
        return lax.all_to_all(parts, "space", 0, 0, tiled=True)

    def work(height):
        accs = [pltpu.VMEM((frames - 2 + i, height, columns, channels), F32) for i in range(3)]
        return [pltpu.VMEM((frames, height + 2, columns, 3 * channels), BF16)] + accs

    above = lax.ppermute(latent, "space", [(i, (i + 1) % bands) for i in range(bands)])
    below = lax.ppermute(latent, "space", [((i + 1) % bands, i) for i in range(bands)])
    vectors = [row(v) for v in (group_of, gain_first, shift_first, bias_first, gain_second, shift_second, bias_second)]
    outs = [parts_out, (latent.shape, BF16), (clip_frames.shape, jnp.int32), (clip_rank.shape, jnp.int32)]
    outs += [(v.shape, v.dtype) for v in vectors]
    parts, latent, clip_frames, clip_rank, *vectors = call(
        stats_kernel, [HBM] * (3 + len(vectors)), outs,
        [pltpu.SMEM(clip_frames.shape, jnp.int32), pltpu.SemaphoreType.DMA((4 + len(vectors),))],
        cost=pl.CostEstimate(flops=1 << 32, bytes_accessed=1 << 24, transcendentals=0),
    )(*map(in_hbm, (clip_frames, clip_rank, latent, *vectors)))
    group_row = vectors[0]
    parts = gather(parts)
    hidden, parts = call(
        first_kernel, [SMEM] + [VMEM] * 9,
        [((frames, height + 2, columns, channels), BF16), parts_out],
        [pltpu.VMEM(latent.shape, BF16)] + work(height + 2),
    )(clip_frames, parts, latent, above, below, *vectors[:4], taps(conv_first))
    parts = gather(parts)
    half = ((2, height, columns, channels), BF16)
    keep, send = call(second_kernel, [SMEM] * 2 + [VMEM] * 8, [half, half], work(height))(
        clip_frames, clip_rank, parts, hidden, latent, group_row, *vectors[4:], taps(conv_second),
    )
    got = lax.ppermute(send, "tm", [(i, i ^ 1) for i in range(clips)])
    chips = clips // 2
    got = list(call(spread_kernel, [SMEM] * 2 + [VMEM] * 2, [half] * chips)(clip_frames, clip_rank, keep, got))
    for step in range(1, chips):
        along = [(i, (i + 2 * step) % clips) for i in range(clips)]
        got[step] = lax.ppermute(got[step], "tm", along)
    (out,) = call(pick_kernel, [SMEM] * 2 + [ANY] * chips, [half], [pltpu.SemaphoreType.DMA((2,))], HBM)(
        clip_frames, clip_rank, *got
    )
    return out


def solution(mesh):
    placed = (P("tm", "space", None, None), P(), P(), P(), P(), P(), P(), P(), P(), P(), P(), P())
    return jax.shard_map(
        local, mesh=mesh, in_specs=placed, out_specs=P("tm", "space", None, None), check_vma=False
    )
```

```python
import functools

import jax
import jax.numpy as jnp
from jax import lax
from jax.experimental import pallas as pl
from jax.experimental.pallas import tpu as pltpu
from jax.sharding import PartitionSpec as P

G = 32
LANES = 128
EPSILON = 1e-06
F32 = jnp.float32
BF16 = jnp.bfloat16
VMEM = pl.BlockSpec(memory_space=pltpu.VMEM)
SMEM = pl.BlockSpec(memory_space=pltpu.SMEM)
HBM = pl.BlockSpec(memory_space=pltpu.HBM)
ANY = pl.BlockSpec(memory_space=pl.ANY)
LIMIT = 20 * 1024 * 1024


def member_rows(group_row):
    rows = lax.broadcasted_iota(jnp.int32, (LANES, group_row.shape[1]), 0)
    return ((rows == group_row) | (rows - G == group_row)).astype(F32).astype(BF16)


def clip_start_of(frames_ref, rank_ref, clip):
    start = jnp.int32(0)
    for k in range(frames_ref.shape[0]):
        start = start + jnp.where(rank_ref[k] < rank_ref[clip], frames_ref[k], 0)
    return start


def in_thirds(row):
    first = row.astype(BF16)
    row = row - first.astype(F32)
    second = row.astype(BF16)
    return [first, second, (row - second.astype(F32)).astype(BF16)]


def dot_rows(rows, members, side):
    pieces = [piece for row in rows for piece in in_thirds(row)]
    pad = jnp.zeros((16 - len(pieces), pieces[0].shape[1]), BF16)
    left = jnp.concatenate(pieces + [pad], axis=0)
    product = lax.dot_general(left, members, (((1,), (side,)), ((), ())), preferred_element_type=F32)
    return [jnp.sum(product[3 * i : 3 * i + 3], axis=0, keepdims=True) for i in range(len(rows))]


def local_stats(field_ref, length, group_row):
    frames, height, columns, channels = field_ref.shape
    pixels = height * columns
    entries = length.astype(F32) * float(pixels)
    live = [jnp.where(f < length, 1.0, 0.0).astype(F32) for f in range(frames)]
    members = member_rows(group_row)
    share = float(G) / channels

    def frame(f):
        return field_ref[f].astype(F32).reshape(pixels, channels)

    mean = jnp.zeros((1, channels), F32)
    for f in range(frames):
        mean = mean + live[f] * jnp.sum(frame(f), axis=0, keepdims=True)
    mean = mean * (1.0 / entries)
    (group_mean,) = dot_rows([mean], members, 1)
    group_mean = group_mean * share
    lane = lax.broadcasted_iota(jnp.int32, (1, LANES), 1)
    group_mean = jnp.where(lane < G, group_mean, 0.0)
    (mean_back,) = dot_rows([group_mean], members, 0)
    spread = jnp.zeros((1, channels), F32)
    for f in range(frames):
        centred = frame(f) - mean
        spread = spread + live[f] * jnp.sum(centred * centred, axis=0, keepdims=True)
    away = mean - mean_back
    (group_spread,) = dot_rows([spread + away * away * entries], members, 1)
    return jnp.where(lane < G, group_mean, group_spread)


def combine_stats(parts, length, pixels, group_row):
    bands = parts.shape[0]
    channels = group_row.shape[1]
    per_band = length.astype(F32) * float(pixels * (channels // G))
    lane = lax.broadcasted_iota(jnp.int32, (1, LANES), 1)
    sums = jnp.sum(parts, axis=0, keepdims=True)
    mean = sums * (1.0 / bands)
    away = parts - mean
    between = jnp.sum(away * away, axis=0, keepdims=True) * per_band
    spread = jnp.where(lane < G, between, jnp.where(lane < 2 * G, sums, 0.0))
    mean = jnp.where(lane < G, mean, 0.0)
    mean_back, spread_back = dot_rows([mean, spread], member_rows(group_row), 0)
    return mean_back, lax.rsqrt(spread_back / (per_band * bands) + EPSILON)


def activate(rows, act_ref, slope, offset, f):
    channels = slope.shape[1]
    for r in range(act_ref.shape[1]):
        half = rows(f, r).astype(F32) * slope + offset
        act = half * jnp.tanh(half) + half
        left = jnp.concatenate([act[:1], act[:-1]], axis=0)
        right = jnp.concatenate([act[1:], act[-1:]], axis=0)
        for step, taken in enumerate((left, act, right)):
            act_ref[f, r, :, step * channels : (step + 1) * channels] = taken.astype(BF16)


def convolve(rows, act_ref, weight_ref, acc_refs, slope, offset):
    frames, height, columns, width = act_ref.shape
    height = height - 2
    ready = 0
    for back_step, acc_ref in enumerate(acc_refs):
        used = frames - 2 + back_step
        for f in range(ready, used):
            activate(rows, act_ref, slope, offset, f)
        ready = used
        slabs = [act_ref[:used, j : j + height].reshape(used * height * columns, width) for j in range(3)]
        kernel = weight_ref[3 * back_step : 3 * back_step + 3].reshape(3 * width, -1)
        part = jnp.dot(jnp.concatenate(slabs, axis=1), kernel, preferred_element_type=F32)
        acc_ref[...] = part.reshape(acc_ref.shape)


def frame_sum(acc_refs, f, zero):
    return acc_refs[0][max(f - 2, 0) + zero] + acc_refs[1][max(f - 1, 0) + zero] + acc_refs[2][f + zero]


def band_ends():
    band = lax.axis_index("space")
    return band == 0, band == lax.axis_size("space") - 1


def in_hbm(array):
    return pltpu.with_memory_space_constraint(array, pltpu.HBM)


def stats_kernel(frames_hbm, rank_hbm, latent_hbm, *rest):
    rows = len(rest) // 2 - 3
    rows_hbm, rest = rest[:rows], rest[rows:]
    parts_ref, latent_ref, frames_ref, rank_ref = rest[:4]
    rows_ref, (frames_smem, sem) = rest[4 : 4 + rows], rest[4 + rows :]
    group_ref = rows_ref[0]
    pairs = [(frames_hbm, frames_smem), (latent_hbm, latent_ref)]
    pairs += list(zip(rows_hbm, rows_ref)) + [(frames_hbm, frames_ref), (rank_hbm, rank_ref)]
    copies = [pltpu.make_async_copy(source, target, sem.at[i]) for i, (source, target) in enumerate(pairs)]
    for copy in copies:
        copy.start()
    for copy in copies[:3]:
        copy.wait()
    length = frames_smem[lax.axis_index("tm")]
    row = local_stats(latent_ref, length, group_ref[...])
    parts_ref[...] = jnp.broadcast_to(row[None], parts_ref.shape)
    for copy in copies[3:]:
        copy.wait()


def first_kernel(
    frames_ref, parts_ref, field_ref, above_ref, below_ref, group_ref, gain_ref, shift_ref, bias_ref, weight_ref,
    hidden_ref, out_parts_ref,
    own_ref, act_ref, *acc_refs,
):
    frames, height, columns, channels = field_ref.shape
    length = frames_ref[lax.axis_index("tm")]
    zero = jnp.minimum(length, 0)
    top, bottom = band_ends()
    mean, inverse = combine_stats(parts_ref[:, 0], length, height * columns, group_ref[...])
    slope = inverse * gain_ref[...] * 0.5
    offset = shift_ref[...] * 0.5 - mean * slope

    def rows(f, r):
        if r < 2:
            row = above_ref[f, height - 2 + r]
            return jnp.where(top, field_ref[f, 0], row) if r == 1 else row
        if r >= height + 2:
            row = below_ref[f, r - height - 2]
            return jnp.where(bottom, field_ref[f, height - 1], row) if r == height + 2 else row
        return field_ref[f, r - 2]

    convolve(rows, act_ref, weight_ref, acc_refs, slope, offset)
    for f in range(frames):
        hidden = (frame_sum(acc_refs, f, zero) + bias_ref[...]).astype(BF16)
        hidden_ref[f] = hidden
        own_ref[f] = hidden[1 : height + 1]
    row = local_stats(own_ref, length, group_ref[...])
    out_parts_ref[...] = jnp.broadcast_to(row[None], out_parts_ref.shape)


def second_kernel(
    frames_ref, rank_ref, parts_ref, hidden_ref, latent_ref, group_ref, gain_ref, shift_ref, bias_ref, weight_ref,
    keep_ref, send_ref,
    act_ref, *acc_refs,
):
    frames, height, columns, channels = latent_ref.shape
    clip = lax.axis_index("tm")
    core = lax.rem(clip, 2)
    length = frames_ref[clip]
    zero = jnp.minimum(length, 0)
    start = clip_start_of(frames_ref, rank_ref, clip)
    top, bottom = band_ends()
    mean, inverse = combine_stats(parts_ref[:, 0], length, height * columns, group_ref[...])
    slope = inverse * gain_ref[...] * 0.5
    offset = shift_ref[...] * 0.5 - mean * slope

    def rows(f, r):
        row = hidden_ref[f, r]
        if r == 0:
            return jnp.where(top, hidden_ref[f, 1], row)
        return jnp.where(bottom, hidden_ref[f, height], row) if r == height + 1 else row

    convolve(rows, act_ref, weight_ref, acc_refs, slope, offset)
    for f in range(frames):
        total = (latent_ref[f].astype(F32) + (frame_sum(acc_refs, f, zero) + bias_ref[...])).astype(BF16)
        place = lax.rem(start + f, 4)
        slot = lax.rem(place, 2)
        stays = place // 2 == core

        @pl.when(stays)
        def _():
            keep_ref[slot] = total

        @pl.when(jnp.logical_not(stays))
        def _():
            send_ref[slot] = total


def spread_kernel(frames_ref, rank_ref, keep_ref, got_ref, *out_refs):
    clip = lax.axis_index("tm")
    core = lax.rem(clip, 2)
    chips = len(out_refs)
    other = clip + 1 - 2 * core
    start = clip_start_of(frames_ref, rank_ref, other)
    length = frames_ref[other]
    for step, out_ref in enumerate(out_refs):
        chip = lax.rem(clip // 2 + step, chips)
        for slot in range(2):
            place = 4 * chip + 2 * core + slot - start
            theirs = (place >= 0) & (place < length)
            out_ref[slot] = jnp.where(theirs, got_ref[slot], keep_ref[slot])


def pick_kernel(frames_ref, rank_ref, *rest):
    *got_refs, out_hbm, sem = rest
    clip = lax.axis_index("tm")
    chips = len(got_refs)
    starts = [clip_start_of(frames_ref, rank_ref, k) for k in range(frames_ref.shape[0])]
    copies = []
    for slot in range(2):
        place = 2 * clip + slot
        source = jnp.int32(0)
        for k, start in enumerate(starts):
            source = source + jnp.where((place >= start) & (place < start + frames_ref[k]), k // 2, 0)
        step = lax.rem(clip // 2 - source + chips, chips)
        for k, got_ref in enumerate(got_refs):
            copy = pltpu.make_async_copy(got_ref.at[slot], out_hbm.at[slot], sem.at[slot])
            pl.when(step == k)(copy.start)
        copies.append(copy)
    for copy in copies:
        copy.wait()


def call(kernel, in_specs, outs, scratch=(), out_spec=VMEM, cost=None):
    return pl.pallas_call(
        kernel,
        in_specs=in_specs,
        out_specs=[out_spec] * len(outs),
        out_shape=[jax.ShapeDtypeStruct(shape, kind) for shape, kind in outs],
        scratch_shapes=list(scratch),
        compiler_params=pltpu.CompilerParams(vmem_limit_bytes=LIMIT),
        cost_estimate=cost,
    )


def local(
    latent,
    clip_frames,
    clip_rank,
    group_of,
    gain_first,
    shift_first,
    conv_first,
    bias_first,
    gain_second,
    shift_second,
    conv_second,
    bias_second,
):
    frames, height, columns, channels = latent.shape
    bands = lax.axis_size("space")
    clips = lax.axis_size("tm")
    row = lambda v: v.reshape(1, channels)
    taps = lambda k: k.reshape(9, 3 * channels, channels)
    group_row = row(group_of)
    parts_out = ((bands, 1, LANES), F32)

    def gather(parts):
        return lax.all_to_all(parts, "space", 0, 0, tiled=True)

    def work(height):
        accs = [pltpu.VMEM((frames - 2 + i, height, columns, channels), F32) for i in range(3)]
        return [pltpu.VMEM((frames, height + 2, columns, 3 * channels), BF16)] + accs

    above = lax.ppermute(latent, "space", [(i, (i + 1) % bands) for i in range(bands)])
    below = lax.ppermute(latent, "space", [((i + 1) % bands, i) for i in range(bands)])
    vectors = [row(v) for v in (group_of, gain_first, shift_first, bias_first, gain_second, shift_second, bias_second)]
    outs = [parts_out, (latent.shape, BF16), (clip_frames.shape, jnp.int32), (clip_rank.shape, jnp.int32)]
    outs += [(v.shape, v.dtype) for v in vectors]
    parts, latent, clip_frames, clip_rank, *vectors = call(
        stats_kernel, [HBM] * (3 + len(vectors)), outs,
        [pltpu.SMEM(clip_frames.shape, jnp.int32), pltpu.SemaphoreType.DMA((4 + len(vectors),))],
        cost=pl.CostEstimate(flops=1 << 32, bytes_accessed=1 << 24, transcendentals=0),
    )(*map(in_hbm, (clip_frames, clip_rank, latent, *vectors)))
    group_row = vectors[0]
    parts = gather(parts)
    hidden, parts = call(
        first_kernel, [SMEM] + [VMEM] * 9,
        [((frames, height + 2, columns, channels), BF16), parts_out],
        [pltpu.VMEM(latent.shape, BF16)] + work(height + 2),
    )(clip_frames, parts, latent, above, below, *vectors[:4], taps(conv_first))
    parts = gather(parts)
    half = ((2, height, columns, channels), BF16)
    keep, send = call(second_kernel, [SMEM] * 2 + [VMEM] * 8, [half, half], work(height))(
        clip_frames, clip_rank, parts, hidden, latent, group_row, *vectors[4:], taps(conv_second),
    )
    got = lax.ppermute(send, "tm", [(i, i ^ 1) for i in range(clips)])
    chips = clips // 2
    got = list(call(spread_kernel, [SMEM] * 2 + [VMEM] * 2, [half] * chips)(clip_frames, clip_rank, keep, got))
    for step in range(1, chips):
        along = [(i, (i + 2 * step) % clips) for i in range(clips)]
        got[step] = lax.ppermute(got[step], "tm", along)
    (out,) = call(pick_kernel, [SMEM] * 2 + [ANY] * chips, [half], [pltpu.SemaphoreType.DMA((2,))], HBM)(
        clip_frames, clip_rank, *got
    )
    return out


def solution(mesh):
    placed = (P("tm", "space", None, None), P(), P(), P(), P(), P(), P(), P(), P(), P(), P(), P())
    return jax.shard_map(
        local, mesh=mesh, in_specs=placed, out_specs=P("tm", "space", None, None), check_vma=False
    )
```

```python
import functools

import jax
import jax.numpy as jnp
from jax import lax
from jax.experimental import pallas as pl
from jax.experimental.pallas import tpu as pltpu
from jax.sharding import PartitionSpec as P

G = 32
LANES = 128
EPSILON = 1e-06
F32 = jnp.float32
BF16 = jnp.bfloat16
VMEM = pl.BlockSpec(memory_space=pltpu.VMEM)
SMEM = pl.BlockSpec(memory_space=pltpu.SMEM)
HBM = pl.BlockSpec(memory_space=pltpu.HBM)
ANY = pl.BlockSpec(memory_space=pl.ANY)
LIMIT = 20 * 1024 * 1024


def member_rows(group_row):
    rows = lax.broadcasted_iota(jnp.int32, (LANES, group_row.shape[1]), 0)
    return ((rows == group_row) | (rows - G == group_row)).astype(F32).astype(BF16)


def clip_start_of(frames_ref, rank_ref, clip):
    start = jnp.int32(0)
    for k in range(frames_ref.shape[0]):
        start = start + jnp.where(rank_ref[k] < rank_ref[clip], frames_ref[k], 0)
    return start


def in_thirds(row):
    first = row.astype(BF16)
    row = row - first.astype(F32)
    second = row.astype(BF16)
    return [first, second, (row - second.astype(F32)).astype(BF16)]


def dot_rows(rows, members, side):
    pieces = [piece for row in rows for piece in in_thirds(row)]
    pad = jnp.zeros((16 - len(pieces), pieces[0].shape[1]), BF16)
    left = jnp.concatenate(pieces + [pad], axis=0)
    product = lax.dot_general(left, members, (((1,), (side,)), ((), ())), preferred_element_type=F32)
    return [jnp.sum(product[3 * i : 3 * i + 3], axis=0, keepdims=True) for i in range(len(rows))]


def local_stats(field_ref, length, group_row):
    frames, height, columns, channels = field_ref.shape
    pixels = height * columns
    entries = length.astype(F32) * float(pixels)
    live = [jnp.where(f < length, 1.0, 0.0).astype(F32) for f in range(frames)]
    members = member_rows(group_row)
    share = float(G) / channels

    def frame(f):
        return field_ref[f].astype(F32).reshape(pixels, channels)

    mean = jnp.zeros((1, channels), F32)
    for f in range(frames):
        mean = mean + live[f] * jnp.sum(frame(f), axis=0, keepdims=True)
    mean = mean * (1.0 / entries)
    (group_mean,) = dot_rows([mean], members, 1)
    group_mean = group_mean * share
    lane = lax.broadcasted_iota(jnp.int32, (1, LANES), 1)
    group_mean = jnp.where(lane < G, group_mean, 0.0)
    (mean_back,) = dot_rows([group_mean], members, 0)
    spread = jnp.zeros((1, channels), F32)
    for f in range(frames):
        centred = frame(f) - mean
        spread = spread + live[f] * jnp.sum(centred * centred, axis=0, keepdims=True)
    away = mean - mean_back
    (group_spread,) = dot_rows([spread + away * away * entries], members, 1)
    return jnp.where(lane < G, group_mean, group_spread)


def combine_stats(parts, length, pixels, group_row):
    bands = parts.shape[0]
    channels = group_row.shape[1]
    per_band = length.astype(F32) * float(pixels * (channels // G))
    lane = lax.broadcasted_iota(jnp.int32, (1, LANES), 1)
    sums = jnp.sum(parts, axis=0, keepdims=True)
    mean = sums * (1.0 / bands)
    away = parts - mean
    between = jnp.sum(away * away, axis=0, keepdims=True) * per_band
    spread = jnp.where(lane < G, between, jnp.where(lane < 2 * G, sums, 0.0))
    mean = jnp.where(lane < G, mean, 0.0)
    mean_back, spread_back = dot_rows([mean, spread], member_rows(group_row), 0)
    return mean_back, lax.rsqrt(spread_back / (per_band * bands) + EPSILON)


def activate(rows, act_ref, slope, offset, f):
    channels = slope.shape[1]
    for r in range(act_ref.shape[1]):
        half = rows(f, r).astype(F32) * slope + offset
        act = half * jnp.tanh(half) + half
        left = jnp.concatenate([act[:1], act[:-1]], axis=0)
        right = jnp.concatenate([act[1:], act[-1:]], axis=0)
        for step, taken in enumerate((left, act, right)):
            act_ref[f, r, :, step * channels : (step + 1) * channels] = taken.astype(BF16)


def convolve(rows, act_ref, weight_ref, acc_refs, slope, offset, taken):
    frames, _, columns, width = act_ref.shape
    ready = 0
    for back_step, acc_ref in enumerate(acc_refs):
        used = frames - 2 + back_step
        for f in range(ready, used):
            activate(rows, act_ref, slope, offset, f)
        ready = used
        slabs = []
        for places in taken:
            slab = jnp.concatenate([act_ref[:used, pl.ds(place, 1)] for place in places], axis=1)
            slabs.append(slab.reshape(used * len(places) * columns, width))
        kernel = weight_ref[3 * back_step : 3 * back_step + 3].reshape(3 * width, -1)
        part = jnp.dot(jnp.concatenate(slabs, axis=1), kernel, preferred_element_type=F32)
        acc_ref[...] = part.reshape(acc_ref.shape)


def frame_sum(acc_refs, f, zero):
    return acc_refs[0][max(f - 2, 0) + zero] + acc_refs[1][max(f - 1, 0) + zero] + acc_refs[2][f + zero]


def band_ends():
    band = lax.axis_index("space")
    return band == 0, band == lax.axis_size("space") - 1


def in_hbm(array):
    return pltpu.with_memory_space_constraint(array, pltpu.HBM)


def stats_kernel(frames_hbm, rank_hbm, latent_hbm, *rest):
    rows = len(rest) // 2 - 3
    rows_hbm, rest = rest[:rows], rest[rows:]
    parts_ref, latent_ref, frames_ref, rank_ref = rest[:4]
    rows_ref, (frames_smem, sem) = rest[4 : 4 + rows], rest[4 + rows :]
    group_ref = rows_ref[0]
    pairs = [(frames_hbm, frames_smem), (latent_hbm, latent_ref)]
    pairs += list(zip(rows_hbm, rows_ref)) + [(frames_hbm, frames_ref), (rank_hbm, rank_ref)]
    copies = [pltpu.make_async_copy(source, target, sem.at[i]) for i, (source, target) in enumerate(pairs)]
    for copy in copies:
        copy.start()
    for copy in copies[:3]:
        copy.wait()
    length = frames_smem[lax.axis_index("tm")]
    row = local_stats(latent_ref, length, group_ref[...])
    parts_ref[...] = jnp.broadcast_to(row[None], parts_ref.shape)
    for copy in copies[3:]:
        copy.wait()


def first_kernel(
    frames_ref, parts_ref, field_ref, above_ref, group_ref, gain_ref, shift_ref, bias_ref, weight_ref,
    hidden_ref, out_parts_ref,
    act_ref, *acc_refs,
):
    frames, height, columns, channels = field_ref.shape
    length = frames_ref[lax.axis_index("tm")]
    zero = jnp.minimum(length, 0)
    top, _ = band_ends()
    taken = [(0, jnp.where(top, 2, 1)), (1, 2), (jnp.where(top, 1, 2), 3)]
    mean, inverse = combine_stats(parts_ref[:, 0], length, height * columns, group_ref[...])
    slope = inverse * gain_ref[...] * 0.5
    offset = shift_ref[...] * 0.5 - mean * slope

    def rows(f, r):
        return above_ref[f, r] if r < 2 else field_ref[f, r - 2]

    convolve(rows, act_ref, weight_ref, acc_refs, slope, offset, taken)
    for f in range(frames):
        hidden_ref[f] = (frame_sum(acc_refs, f, zero) + bias_ref[...]).astype(BF16)
    row = local_stats(hidden_ref, length, group_ref[...])
    out_parts_ref[...] = jnp.broadcast_to(row[None], out_parts_ref.shape)


def second_kernel(
    frames_ref, rank_ref, parts_ref, hidden_ref, below_ref, latent_ref, group_ref, gain_ref, shift_ref, bias_ref, weight_ref,
    keep_ref, send_ref,
    act_ref, *acc_refs,
):
    frames, height, columns, channels = latent_ref.shape
    clip = lax.axis_index("tm")
    core = lax.rem(clip, 2)
    length = frames_ref[clip]
    zero = jnp.minimum(length, 0)
    start = clip_start_of(frames_ref, rank_ref, clip)
    top, bottom = band_ends()
    taken = [(jnp.where(top, 1, 0), 1), (1, 2), (2, jnp.where(bottom, 2, 3))]
    mean, inverse = combine_stats(parts_ref[:, 0], length, height * columns, group_ref[...])
    slope = inverse * gain_ref[...] * 0.5
    offset = shift_ref[...] * 0.5 - mean * slope

    def rows(f, r):
        return hidden_ref[f, r] if r < 2 else below_ref[f, r - 2]

    convolve(rows, act_ref, weight_ref, acc_refs, slope, offset, taken)
    for f in range(frames):
        total = (latent_ref[f].astype(F32) + (frame_sum(acc_refs, f, zero) + bias_ref[...])).astype(BF16)
        place = lax.rem(start + f, 4)
        slot = lax.rem(place, 2)
        stays = place // 2 == core

        @pl.when(stays)
        def _():
            keep_ref[slot] = total

        @pl.when(jnp.logical_not(stays))
        def _():
            send_ref[slot] = total


def spread_kernel(frames_ref, rank_ref, keep_ref, got_ref, *out_refs):
    clip = lax.axis_index("tm")
    core = lax.rem(clip, 2)
    chips = len(out_refs)
    other = clip + 1 - 2 * core
    start = clip_start_of(frames_ref, rank_ref, other)
    length = frames_ref[other]
    for step, out_ref in enumerate(out_refs):
        chip = lax.rem(clip // 2 + step, chips)
        for slot in range(2):
            place = 4 * chip + 2 * core + slot - start
            theirs = (place >= 0) & (place < length)
            out_ref[slot] = jnp.where(theirs, got_ref[slot], keep_ref[slot])


def pick_kernel(frames_ref, rank_ref, *rest):
    *got_refs, out_hbm, sem = rest
    clip = lax.axis_index("tm")
    chips = len(got_refs)
    starts = [clip_start_of(frames_ref, rank_ref, k) for k in range(frames_ref.shape[0])]
    copies = []
    for slot in range(2):
        place = 2 * clip + slot
        source = jnp.int32(0)
        for k, start in enumerate(starts):
            source = source + jnp.where((place >= start) & (place < start + frames_ref[k]), k // 2, 0)
        step = lax.rem(clip // 2 - source + chips, chips)
        for k, got_ref in enumerate(got_refs):
            copy = pltpu.make_async_copy(got_ref.at[slot], out_hbm.at[slot], sem.at[slot])
            pl.when(step == k)(copy.start)
        copies.append(copy)
    for copy in copies:
        copy.wait()


def call(kernel, in_specs, outs, scratch=(), out_spec=VMEM, cost=None):
    return pl.pallas_call(
        kernel,
        in_specs=in_specs,
        out_specs=[out_spec] * len(outs),
        out_shape=[jax.ShapeDtypeStruct(shape, kind) for shape, kind in outs],
        scratch_shapes=list(scratch),
        compiler_params=pltpu.CompilerParams(vmem_limit_bytes=LIMIT),
        cost_estimate=cost,
    )


def local(
    latent,
    clip_frames,
    clip_rank,
    group_of,
    gain_first,
    shift_first,
    conv_first,
    bias_first,
    gain_second,
    shift_second,
    conv_second,
    bias_second,
):
    frames, height, columns, channels = latent.shape
    bands = lax.axis_size("space")
    clips = lax.axis_size("tm")
    row = lambda v: v.reshape(1, channels)
    taps = lambda k: k.reshape(9, 3 * channels, channels)
    group_row = row(group_of)
    parts_out = ((bands, 1, LANES), F32)

    def gather(parts):
        return lax.all_to_all(parts, "space", 0, 0, tiled=True)

    work = [pltpu.VMEM((frames, 4, columns, 3 * channels), BF16)]
    work += [pltpu.VMEM((frames - 2 + i, height, columns, channels), F32) for i in range(3)]

    above = lax.ppermute(latent, "space", [(i, (i + 1) % bands) for i in range(bands)])
    vectors = [row(v) for v in (group_of, gain_first, shift_first, bias_first, gain_second, shift_second, bias_second)]
    outs = [parts_out, (latent.shape, BF16), (clip_frames.shape, jnp.int32), (clip_rank.shape, jnp.int32)]
    outs += [(v.shape, v.dtype) for v in vectors]
    parts, latent, clip_frames, clip_rank, *vectors = call(
        stats_kernel, [HBM] * (3 + len(vectors)), outs,
        [pltpu.SMEM(clip_frames.shape, jnp.int32), pltpu.SemaphoreType.DMA((4 + len(vectors),))],
        cost=pl.CostEstimate(flops=1 << 32, bytes_accessed=1 << 24, transcendentals=0),
    )(*map(in_hbm, (clip_frames, clip_rank, latent, *vectors)))
    group_row = vectors[0]
    parts = gather(parts)
    hidden, parts = call(first_kernel, [SMEM] + [VMEM] * 8, [(latent.shape, BF16), parts_out], work)(
        clip_frames, parts, latent, above, *vectors[:4], taps(conv_first)
    )
    below = lax.ppermute(hidden, "space", [((i + 1) % bands, i) for i in range(bands)])
    parts = gather(parts)
    half = ((2, height, columns, channels), BF16)
    keep, send = call(second_kernel, [SMEM] * 2 + [VMEM] * 9, [half, half], work)(
        clip_frames, clip_rank, parts, hidden, below, latent, group_row, *vectors[4:], taps(conv_second),
    )
    got = lax.ppermute(send, "tm", [(i, i ^ 1) for i in range(clips)])
    chips = clips // 2
    got = list(call(spread_kernel, [SMEM] * 2 + [VMEM] * 2, [half] * chips)(clip_frames, clip_rank, keep, got))
    for step in range(1, chips):
        along = [(i, (i + 2 * step) % clips) for i in range(clips)]
        got[step] = lax.ppermute(got[step], "tm", along)
    (out,) = call(pick_kernel, [SMEM] * 2 + [ANY] * chips, [half], [pltpu.SemaphoreType.DMA((2,))], HBM)(
        clip_frames, clip_rank, *got
    )
    return out


def solution(mesh):
    placed = (P("tm", "space", None, None), P(), P(), P(), P(), P(), P(), P(), P(), P(), P(), P())
    return jax.shard_map(
        local, mesh=mesh, in_specs=placed, out_specs=P("tm", "space", None, None), check_vma=False
    )
```

```python
import functools

import jax
import jax.numpy as jnp
from jax import lax
from jax.experimental import pallas as pl
from jax.experimental.pallas import tpu as pltpu
from jax.sharding import PartitionSpec as P

G = 32
LANES = 128
EPSILON = 1e-06
F32 = jnp.float32
BF16 = jnp.bfloat16
VMEM = pl.BlockSpec(memory_space=pltpu.VMEM)
SMEM = pl.BlockSpec(memory_space=pltpu.SMEM)
HBM = pl.BlockSpec(memory_space=pltpu.HBM)
ANY = pl.BlockSpec(memory_space=pl.ANY)
LIMIT = 20 * 1024 * 1024


def member_rows(group_row):
    rows = lax.broadcasted_iota(jnp.int32, (LANES, group_row.shape[1]), 0)
    return ((rows == group_row) | (rows - G == group_row)).astype(F32).astype(BF16)


def clip_start_of(frames_ref, rank_ref, clip):
    start = jnp.int32(0)
    for k in range(frames_ref.shape[0]):
        start = start + jnp.where(rank_ref[k] < rank_ref[clip], frames_ref[k], 0)
    return start


def in_thirds(row):
    first = row.astype(BF16)
    row = row - first.astype(F32)
    second = row.astype(BF16)
    return [first, second, (row - second.astype(F32)).astype(BF16)]


def dot_rows(rows, members, side):
    pieces = [piece for row in rows for piece in in_thirds(row)]
    pad = jnp.zeros((16 - len(pieces), pieces[0].shape[1]), BF16)
    left = jnp.concatenate(pieces + [pad], axis=0)
    product = lax.dot_general(left, members, (((1,), (side,)), ((), ())), preferred_element_type=F32)
    return [jnp.sum(product[3 * i : 3 * i + 3], axis=0, keepdims=True) for i in range(len(rows))]


def local_stats(field_ref, length_row, group_row):
    frames, height, columns, channels = field_ref.shape
    pixels = height * columns
    entries = length_row * float(pixels)
    live = [jnp.where(length_row > f, 1.0, 0.0) for f in range(frames)]
    members = member_rows(group_row)
    share = float(G) / channels

    def frame(f):
        return field_ref[f].astype(F32).reshape(pixels, channels)

    mean = jnp.zeros((1, channels), F32)
    for f in range(frames):
        mean = mean + live[f] * jnp.sum(frame(f), axis=0, keepdims=True)
    mean = mean * (1.0 / entries)
    (group_mean,) = dot_rows([mean], members, 1)
    group_mean = group_mean * share
    lane = lax.broadcasted_iota(jnp.int32, (1, LANES), 1)
    group_mean = jnp.where(lane < G, group_mean, 0.0)
    (mean_back,) = dot_rows([group_mean], members, 0)
    spread = jnp.zeros((1, channels), F32)
    for f in range(frames):
        centred = frame(f) - mean
        spread = spread + live[f] * jnp.sum(centred * centred, axis=0, keepdims=True)
    away = mean - mean_back
    (group_spread,) = dot_rows([spread + away * away * entries], members, 1)
    return jnp.where(lane < G, group_mean, group_spread)


def combine_stats(parts, length_row, pixels, group_row):
    bands = parts.shape[0]
    channels = group_row.shape[1]
    per_band = length_row * float(pixels * (channels // G))
    lane = lax.broadcasted_iota(jnp.int32, (1, LANES), 1)
    sums = jnp.sum(parts, axis=0, keepdims=True)
    mean = sums * (1.0 / bands)
    away = parts - mean
    between = jnp.sum(away * away, axis=0, keepdims=True) * per_band[:, :LANES]
    spread = jnp.where(lane < G, between, jnp.where(lane < 2 * G, sums, 0.0))
    mean = jnp.where(lane < G, mean, 0.0)
    mean_back, spread_back = dot_rows([mean, spread], member_rows(group_row), 0)
    return mean_back, lax.rsqrt(spread_back / (per_band * bands) + EPSILON)


def activate(rows, act_ref, slope, offset, f):
    channels = slope.shape[1]
    for r in range(act_ref.shape[0]):
        half = rows(f, r).astype(F32) * slope + offset
        act = half * jnp.tanh(half) + half
        left = jnp.concatenate([act[:1], act[:-1]], axis=0)
        right = jnp.concatenate([act[1:], act[-1:]], axis=0)
        for step, taken in enumerate((left, act, right)):
            act_ref[r, :, step * channels : (step + 1) * channels] = taken.astype(BF16)


def convolve(rows, act_refs, weight_ref, acc_refs, slope, offset, taken):
    frames = len(act_refs)
    _, columns, width = act_refs[0].shape
    ready = 0
    for back_step, acc_ref in enumerate(acc_refs):
        used = frames - 2 + back_step
        for f in range(ready, used):
            activate(rows, act_refs[f], slope, offset, f)
        ready = used
        slabs = []
        for places in taken:
            pieces = [act_refs[f][place] for f in range(used) for place in places]
            slabs.append(jnp.concatenate(pieces, axis=0))
        kernel = weight_ref[3 * back_step : 3 * back_step + 3].reshape(3 * width, -1)
        part = jnp.dot(jnp.concatenate(slabs, axis=1), kernel, preferred_element_type=F32)
        acc_ref[...] = part.reshape(acc_ref.shape)


def frame_sum(acc_refs, f, zero):
    return acc_refs[0][max(f - 2, 0) + zero] + acc_refs[1][max(f - 1, 0) + zero] + acc_refs[2][f + zero]


def band_ends():
    band = lax.axis_index("space")
    return band == 0, band == lax.axis_size("space") - 1


def in_hbm(array):
    return pltpu.with_memory_space_constraint(array, pltpu.HBM)


def plan_row(frames_ref, rank_ref):
    count = frames_ref.shape[0]
    starts = [clip_start_of(frames_ref, rank_ref, k) for k in range(count)]
    clip = lax.axis_index("tm")
    core = lax.rem(clip, 2)
    other = clip + 1 - 2 * core
    chips = count // 2

    def entry(values, index):
        taken = jnp.int32(0)
        for k, value in enumerate(values):
            taken = taken + jnp.where(index == k, value, 0)
        return taken

    plan = [lax.rem(entry(starts, clip), 4), entry(starts, other), frames_ref[other]]
    for slot in range(2):
        place = 2 * clip + slot
        source = jnp.int32(0)
        for k, start in enumerate(starts):
            source = source + jnp.where((place >= start) & (place < start + frames_ref[k]), k // 2, 0)
        plan.append(lax.rem(clip // 2 - source + chips, chips))
    lane = lax.broadcasted_iota(jnp.int32, (1, LANES), 1)
    row = jnp.zeros((1, LANES), jnp.int32)
    for k, value in enumerate(plan):
        row = jnp.where(lane == k, value, row)
    return row


def stats_kernel(frames_hbm, rank_hbm, latent_hbm, *rest):
    rows = len(rest) // 2 - 3
    rows_hbm, rest = rest[:rows], rest[rows:]
    parts_ref, latent_ref, plan_ref, length_ref = rest[:4]
    rows_ref, (frames_ref, rank_ref, sem) = rest[4 : 4 + rows], rest[4 + rows :]
    group_ref = rows_ref[0]
    pairs = [(frames_hbm, frames_ref), (rank_hbm, rank_ref), (latent_hbm, latent_ref)] + list(zip(rows_hbm, rows_ref))
    copies = [pltpu.make_async_copy(source, target, sem.at[i]) for i, (source, target) in enumerate(pairs)]
    for copy in copies:
        copy.start()
    for copy in copies[:4]:
        copy.wait()
    length = frames_ref[lax.axis_index("tm")].astype(F32)
    length_row = jnp.full(length_ref.shape, length, F32)
    length_ref[...] = length_row
    row = local_stats(latent_ref, length_row, group_ref[...])
    parts_ref[...] = jnp.broadcast_to(row[None], parts_ref.shape)
    plan_ref[...] = plan_row(frames_ref, rank_ref)
    for copy in copies[4:]:
        copy.wait()


def first_kernel(
    length_ref, parts_ref, field_ref, above_ref, group_ref, gain_ref, shift_ref, bias_ref, weight_ref,
    hidden_ref, out_parts_ref,
    *work_refs,
):
    frames, height, columns, channels = field_ref.shape
    zero = jnp.minimum(lax.axis_index("tm"), 0)
    top, _ = band_ends()
    taken = [(0, jnp.where(top, 2, 1)), (1, 2), (jnp.where(top, 1, 2), 3)]
    mean, inverse = combine_stats(parts_ref[:, 0], length_ref[...], height * columns, group_ref[...])
    slope = inverse * gain_ref[...] * 0.5
    offset = shift_ref[...] * 0.5 - mean * slope

    def rows(f, r):
        return above_ref[f, r] if r < 2 else field_ref[f, r - 2]

    act_refs, acc_refs = work_refs[:frames], work_refs[frames:]
    convolve(rows, act_refs, weight_ref, acc_refs, slope, offset, taken)
    for f in range(frames):
        hidden_ref[f] = (frame_sum(acc_refs, f, zero) + bias_ref[...]).astype(BF16)
    row = local_stats(hidden_ref, length_ref[...], group_ref[...])
    out_parts_ref[...] = jnp.broadcast_to(row[None], out_parts_ref.shape)


def second_kernel(
    plan_vmem, length_ref, parts_ref, hidden_ref, below_ref, latent_ref, group_ref, gain_ref, shift_ref, bias_ref,
    weight_ref,
    keep_ref, send_ref,
    plan_ref, sem, *work_refs,
):
    plan_copy = pltpu.make_async_copy(plan_vmem, plan_ref, sem)
    plan_copy.start()
    frames, height, columns, channels = latent_ref.shape
    clip = lax.axis_index("tm")
    core = lax.rem(clip, 2)
    zero = jnp.minimum(clip, 0)
    top, bottom = band_ends()
    taken = [(jnp.where(top, 1, 0), 1), (1, 2), (2, jnp.where(bottom, 2, 3))]
    mean, inverse = combine_stats(parts_ref[:, 0], length_ref[...], height * columns, group_ref[...])
    slope = inverse * gain_ref[...] * 0.5
    offset = shift_ref[...] * 0.5 - mean * slope

    def rows(f, r):
        return hidden_ref[f, r] if r < 2 else below_ref[f, r - 2]

    act_refs, acc_refs = work_refs[:frames], work_refs[frames:]
    convolve(rows, act_refs, weight_ref, acc_refs, slope, offset, taken)
    plan_copy.wait()
    for f in range(frames):
        total = (latent_ref[f].astype(F32) + (frame_sum(acc_refs, f, zero) + bias_ref[...])).astype(BF16)
        place = lax.rem(plan_ref[0, 0] + f, 4)
        slot = lax.rem(place, 2)
        stays = place // 2 == core

        @pl.when(stays)
        def _():
            keep_ref[slot] = total

        @pl.when(jnp.logical_not(stays))
        def _():
            send_ref[slot] = total


def spread_kernel(plan_ref, keep_ref, got_ref, *out_refs):
    clip = lax.axis_index("tm")
    core = lax.rem(clip, 2)
    chips = len(out_refs)
    start, length = plan_ref[0, 1], plan_ref[0, 2]
    for step, out_ref in enumerate(out_refs):
        chip = lax.rem(clip // 2 + step, chips)
        for slot in range(2):
            place = 4 * chip + 2 * core + slot - start
            theirs = (place >= 0) & (place < length)
            out_ref[slot] = jnp.where(theirs, got_ref[slot], keep_ref[slot])


def pick_kernel(plan_ref, *rest):
    *got_refs, out_hbm, sem = rest
    copies = []
    for slot in range(2):
        step = plan_ref[0, 3 + slot]
        for k, got_ref in enumerate(got_refs):
            copy = pltpu.make_async_copy(got_ref.at[slot], out_hbm.at[slot], sem.at[slot])
            pl.when(step == k)(copy.start)
        copies.append(copy)
    for copy in copies:
        copy.wait()


def call(kernel, in_specs, outs, scratch=(), out_spec=VMEM, cost=None):
    return pl.pallas_call(
        kernel,
        in_specs=in_specs,
        out_specs=[out_spec] * len(outs),
        out_shape=[jax.ShapeDtypeStruct(shape, kind) for shape, kind in outs],
        scratch_shapes=list(scratch),
        compiler_params=pltpu.CompilerParams(vmem_limit_bytes=LIMIT),
        cost_estimate=cost,
    )


def local(
    latent,
    clip_frames,
    clip_rank,
    group_of,
    gain_first,
    shift_first,
    conv_first,
    bias_first,
    gain_second,
    shift_second,
    conv_second,
    bias_second,
):
    frames, height, columns, channels = latent.shape
    bands = lax.axis_size("space")
    clips = lax.axis_size("tm")
    row = lambda v: v.reshape(1, channels)
    taps = lambda k: k.reshape(9, 3 * channels, channels)
    group_row = row(group_of)
    parts_out = ((bands, 1, LANES), F32)

    def gather(parts):
        return lax.all_to_all(parts, "space", 0, 0, tiled=True)

    work = [pltpu.VMEM((4, columns, 3 * channels), BF16)] * frames
    work += [pltpu.VMEM((frames - 2 + i, height, columns, channels), F32) for i in range(3)]

    above = lax.ppermute(latent, "space", [(i, (i + 1) % bands) for i in range(bands)])
    vectors = [row(v) for v in (group_of, gain_first, shift_first, bias_first, gain_second, shift_second, bias_second)]
    outs = [parts_out, (latent.shape, BF16), ((1, LANES), jnp.int32), ((1, channels), F32)]
    outs += [(v.shape, v.dtype) for v in vectors]
    scalars = pltpu.SMEM(clip_frames.shape, jnp.int32)
    parts, latent, plan, length, *vectors = call(
        stats_kernel, [HBM] * (3 + len(vectors)), outs,
        [scalars, scalars, pltpu.SemaphoreType.DMA((3 + len(vectors),))],
        cost=pl.CostEstimate(flops=1 << 32, bytes_accessed=1 << 24, transcendentals=0),
    )(*map(in_hbm, (clip_frames, clip_rank, latent, *vectors)))
    group_row = vectors[0]
    parts = gather(parts)
    hidden, parts = call(first_kernel, [VMEM] * 9, [(latent.shape, BF16), parts_out], work)(
        length, parts, latent, above, *vectors[:4], taps(conv_first)
    )
    below = lax.ppermute(hidden, "space", [((i + 1) % bands, i) for i in range(bands)])
    parts = gather(parts)
    half = ((2, height, columns, channels), BF16)
    work = [pltpu.SMEM(plan.shape, jnp.int32), pltpu.SemaphoreType.DMA] + work
    keep, send = call(second_kernel, [ANY] + [VMEM] * 10, [half, half], work)(
        plan, length, parts, hidden, below, latent, group_row, *vectors[4:], taps(conv_second),
    )
    got = lax.ppermute(send, "tm", [(i, i ^ 1) for i in range(clips)])
    chips = clips // 2
    got = list(call(spread_kernel, [SMEM] + [VMEM] * 2, [half] * chips)(plan, keep, got))
    for step in range(1, chips):
        along = [(i, (i + 2 * step) % clips) for i in range(clips)]
        got[step] = lax.ppermute(got[step], "tm", along)
    (out,) = call(pick_kernel, [SMEM] + [ANY] * chips, [half], [pltpu.SemaphoreType.DMA((2,))], HBM)(plan, *got)
    return out


def solution(mesh):
    placed = (P("tm", "space", None, None), P(), P(), P(), P(), P(), P(), P(), P(), P(), P(), P())
    return jax.shard_map(
        local, mesh=mesh, in_specs=placed, out_specs=P("tm", "space", None, None), check_vma=False
    )
```

```python
import functools

import jax
import jax.numpy as jnp
from jax import lax
from jax.experimental import pallas as pl
from jax.experimental.pallas import tpu as pltpu
from jax.sharding import PartitionSpec as P

G = 32
LANES = 128
EPSILON = 1e-06
F32 = jnp.float32
BF16 = jnp.bfloat16
VMEM = pl.BlockSpec(memory_space=pltpu.VMEM)
SMEM = pl.BlockSpec(memory_space=pltpu.SMEM)
HBM = pl.BlockSpec(memory_space=pltpu.HBM)
ANY = pl.BlockSpec(memory_space=pl.ANY)
LIMIT = 20 * 1024 * 1024


def member_rows(group_row):
    rows = lax.broadcasted_iota(jnp.int32, (LANES, group_row.shape[1]), 0)
    return ((rows == group_row) | (rows - G == group_row)).astype(F32).astype(BF16)


def clip_start_of(frames_ref, rank_ref, clip):
    start = jnp.int32(0)
    for k in range(frames_ref.shape[0]):
        start = start + jnp.where(rank_ref[k] < rank_ref[clip], frames_ref[k], 0)
    return start


def in_thirds(row):
    first = row.astype(BF16)
    row = row - first.astype(F32)
    second = row.astype(BF16)
    return [first, second, (row - second.astype(F32)).astype(BF16)]


def dot_rows(rows, members, side):
    pieces = [piece for row in rows for piece in in_thirds(row)]
    pad = jnp.zeros((16 - len(pieces), pieces[0].shape[1]), BF16)
    left = jnp.concatenate(pieces + [pad], axis=0)
    product = lax.dot_general(left, members, (((1,), (side,)), ((), ())), preferred_element_type=F32)
    return [jnp.sum(product[3 * i : 3 * i + 3], axis=0, keepdims=True) for i in range(len(rows))]


def local_stats(field_ref, length_row, group_row):
    frames, height, columns, channels = field_ref.shape
    pixels = height * columns
    entries = length_row * float(pixels)
    live = [jnp.where(length_row > f, 1.0, 0.0) for f in range(frames)]
    members = member_rows(group_row)
    share = float(G) / channels

    def frame(f):
        return field_ref[f].astype(F32).reshape(pixels, channels)

    mean = jnp.zeros((1, channels), F32)
    for f in range(frames):
        mean = mean + live[f] * jnp.sum(frame(f), axis=0, keepdims=True)
    mean = mean * (1.0 / entries)
    (group_mean,) = dot_rows([mean], members, 1)
    group_mean = group_mean * share
    lane = lax.broadcasted_iota(jnp.int32, (1, LANES), 1)
    group_mean = jnp.where(lane < G, group_mean, 0.0)
    (mean_back,) = dot_rows([group_mean], members, 0)
    spread = jnp.zeros((1, channels), F32)
    for f in range(frames):
        centred = frame(f) - mean
        spread = spread + live[f] * jnp.sum(centred * centred, axis=0, keepdims=True)
    away = mean - mean_back
    (group_spread,) = dot_rows([spread + away * away * entries], members, 1)
    return jnp.where(lane < G, group_mean, group_spread)


def combine_stats(parts, length_row, pixels, group_row):
    bands = parts.shape[0]
    channels = group_row.shape[1]
    per_band = length_row * float(pixels * (channels // G))
    lane = lax.broadcasted_iota(jnp.int32, (1, LANES), 1)
    sums = jnp.sum(parts, axis=0, keepdims=True)
    mean = sums * (1.0 / bands)
    away = parts - mean
    between = jnp.sum(away * away, axis=0, keepdims=True) * per_band[:, :LANES]
    spread = jnp.where(lane < G, between, jnp.where(lane < 2 * G, sums, 0.0))
    mean = jnp.where(lane < G, mean, 0.0)
    mean_back, spread_back = dot_rows([mean, spread], member_rows(group_row), 0)
    return mean_back, lax.rsqrt(spread_back / (per_band * bands) + EPSILON)


def activate(rows, act_ref, slope, offset, f):
    channels = slope.shape[1]
    for r in range(act_ref.shape[0]):
        half = rows(f, r).astype(F32) * slope + offset
        act = half * jnp.tanh(half) + half
        left = jnp.concatenate([act[:1], act[:-1]], axis=0)
        right = jnp.concatenate([act[1:], act[-1:]], axis=0)
        for step, taken in enumerate((left, act, right)):
            act_ref[r, :, step * channels : (step + 1) * channels] = taken.astype(BF16)


def convolve(rows, act_refs, weight_ref, acc_refs, slope, offset, taken):
    frames = len(act_refs)
    _, columns, width = act_refs[0].shape
    ready = 0
    for back_step, acc_ref in enumerate(acc_refs):
        used = frames - 2 + back_step
        for f in range(ready, used):
            activate(rows, act_refs[f], slope, offset, f)
        ready = used
        slabs = []
        for places in taken:
            pieces = [act_refs[f][place] for f in range(used) for place in places]
            slabs.append(jnp.concatenate(pieces, axis=0))
        kernel = weight_ref[3 * back_step : 3 * back_step + 3].reshape(3 * width, -1)
        part = jnp.dot(jnp.concatenate(slabs, axis=1), kernel, preferred_element_type=F32)
        acc_ref[...] = part.reshape(acc_ref.shape)


def frame_sum(acc_refs, f, zero):
    return acc_refs[0][max(f - 2, 0) + zero] + acc_refs[1][max(f - 1, 0) + zero] + acc_refs[2][f + zero]


def band_ends():
    band = lax.axis_index("space")
    return band == 0, band == lax.axis_size("space") - 1


def in_hbm(array):
    return pltpu.with_memory_space_constraint(array, pltpu.HBM)


def in_smem(array):
    return pltpu.with_memory_space_constraint(array, pltpu.SMEM)


def plan_of(frames_ref, rank_ref):
    count = frames_ref.shape[0]
    starts = [clip_start_of(frames_ref, rank_ref, k) for k in range(count)]
    clip = lax.axis_index("tm")
    core = lax.rem(clip, 2)
    other = clip + 1 - 2 * core
    chips = count // 2

    def entry(values, index):
        taken = jnp.int32(0)
        for k, value in enumerate(values):
            taken = taken + jnp.where(index == k, value, 0)
        return taken

    plan = [lax.rem(entry(starts, clip), 4), entry(starts, other), frames_ref[other]]
    for slot in range(2):
        place = 2 * clip + slot
        source = jnp.int32(0)
        for k, start in enumerate(starts):
            source = source + jnp.where((place >= start) & (place < start + frames_ref[k]), k // 2, 0)
        plan.append(lax.rem(clip // 2 - source + chips, chips))
    return plan


def stats_kernel(frames_hbm, rank_hbm, latent_hbm, *rest):
    rows = len(rest) // 2 - 3
    rows_hbm, rest = rest[:rows], rest[rows:]
    parts_ref, latent_ref, plan_ref, length_ref = rest[:4]
    rows_ref, (frames_ref, rank_ref, sem) = rest[4 : 4 + rows], rest[4 + rows :]
    group_ref = rows_ref[0]
    pairs = [(frames_hbm, frames_ref), (rank_hbm, rank_ref), (latent_hbm, latent_ref)] + list(zip(rows_hbm, rows_ref))
    copies = [pltpu.make_async_copy(source, target, sem.at[i]) for i, (source, target) in enumerate(pairs)]
    for copy in copies:
        copy.start()
    for copy in copies[:4]:
        copy.wait()
    length = frames_ref[lax.axis_index("tm")].astype(F32)
    length_row = jnp.full(length_ref.shape, length, F32)
    length_ref[...] = length_row
    row = local_stats(latent_ref, length_row, group_ref[...])
    parts_ref[...] = jnp.broadcast_to(row[None], parts_ref.shape)
    for k, value in enumerate(plan_of(frames_ref, rank_ref)):
        plan_ref[k] = value
    for copy in copies[4:]:
        copy.wait()


def first_kernel(
    plan_ref, length_ref, parts_ref, field_ref, above_ref, group_ref, gain_ref, shift_ref, bias_ref, weight_ref,
    hidden_ref, out_parts_ref,
    *work_refs,
):
    frames, height, columns, channels = field_ref.shape
    zero = jnp.minimum(plan_ref[0], 0)
    top, _ = band_ends()
    taken = [(0, jnp.where(top, 2, 1)), (1, 2), (jnp.where(top, 1, 2), 3)]
    mean, inverse = combine_stats(parts_ref[:, 0], length_ref[...], height * columns, group_ref[...])
    slope = inverse * gain_ref[...] * 0.5
    offset = shift_ref[...] * 0.5 - mean * slope

    def rows(f, r):
        return above_ref[f, r] if r < 2 else field_ref[f, r - 2]

    act_refs, acc_refs = work_refs[:frames], work_refs[frames:]
    convolve(rows, act_refs, weight_ref, acc_refs, slope, offset, taken)
    for f in range(frames):
        hidden_ref[f] = (frame_sum(acc_refs, f, zero) + bias_ref[...]).astype(BF16)
    row = local_stats(hidden_ref, length_ref[...], group_ref[...])
    out_parts_ref[...] = jnp.broadcast_to(row[None], out_parts_ref.shape)


def second_kernel(
    plan_ref, length_ref, parts_ref, hidden_ref, below_ref, latent_ref, group_ref, gain_ref, shift_ref, bias_ref,
    weight_ref,
    keep_ref, send_ref,
    *work_refs,
):
    frames, height, columns, channels = latent_ref.shape
    core = lax.rem(lax.axis_index("tm"), 2)
    zero = jnp.minimum(plan_ref[0], 0)
    top, bottom = band_ends()
    taken = [(jnp.where(top, 1, 0), 1), (1, 2), (2, jnp.where(bottom, 2, 3))]
    mean, inverse = combine_stats(parts_ref[:, 0], length_ref[...], height * columns, group_ref[...])
    slope = inverse * gain_ref[...] * 0.5
    offset = shift_ref[...] * 0.5 - mean * slope

    def rows(f, r):
        return hidden_ref[f, r] if r < 2 else below_ref[f, r - 2]

    act_refs, acc_refs = work_refs[:frames], work_refs[frames:]
    convolve(rows, act_refs, weight_ref, acc_refs, slope, offset, taken)
    for f in range(frames):
        total = (latent_ref[f].astype(F32) + (frame_sum(acc_refs, f, zero) + bias_ref[...])).astype(BF16)
        place = lax.rem(plan_ref[0] + f, 4)
        slot = lax.rem(place, 2)
        stays = place // 2 == core

        @pl.when(stays)
        def _():
            keep_ref[slot] = total

        @pl.when(jnp.logical_not(stays))
        def _():
            send_ref[slot] = total


def spread_kernel(plan_ref, keep_ref, got_ref, *out_refs):
    clip = lax.axis_index("tm")
    core = lax.rem(clip, 2)
    chips = len(out_refs)
    start, length = plan_ref[1], plan_ref[2]
    for step, out_ref in enumerate(out_refs):
        chip = lax.rem(clip // 2 + step, chips)
        for slot in range(2):
            place = 4 * chip + 2 * core + slot - start
            theirs = (place >= 0) & (place < length)
            out_ref[slot] = jnp.where(theirs, got_ref[slot], keep_ref[slot])


def pick_kernel(plan_ref, *rest):
    *got_refs, out_hbm, sem = rest
    copies = []
    for slot in range(2):
        step = plan_ref[3 + slot]
        for k, got_ref in enumerate(got_refs):
            copy = pltpu.make_async_copy(got_ref.at[slot], out_hbm.at[slot], sem.at[slot])
            pl.when(step == k)(copy.start)
        copies.append(copy)
    for copy in copies:
        copy.wait()


def call(kernel, in_specs, outs, scratch=(), out_spec=VMEM, cost=None):
    return pl.pallas_call(
        kernel,
        in_specs=in_specs,
        out_specs=[out_spec if isinstance(out, tuple) else SMEM for out in outs],
        out_shape=[jax.ShapeDtypeStruct(*out) if isinstance(out, tuple) else out for out in outs],
        scratch_shapes=list(scratch),
        compiler_params=pltpu.CompilerParams(vmem_limit_bytes=LIMIT),
        cost_estimate=cost,
    )


def local(
    latent,
    clip_frames,
    clip_rank,
    group_of,
    gain_first,
    shift_first,
    conv_first,
    bias_first,
    gain_second,
    shift_second,
    conv_second,
    bias_second,
):
    frames, height, columns, channels = latent.shape
    bands = lax.axis_size("space")
    clips = lax.axis_size("tm")
    row = lambda v: v.reshape(1, channels)
    taps = lambda k: k.reshape(9, 3 * channels, channels)
    group_row = row(group_of)
    parts_out = ((bands, 1, LANES), F32)

    def gather(parts):
        return lax.all_to_all(parts, "space", 0, 0, tiled=True)

    work = [pltpu.VMEM((4, columns, 3 * channels), BF16)] * frames
    work += [pltpu.VMEM((frames - 2 + i, height, columns, channels), F32) for i in range(3)]

    above = lax.ppermute(latent, "space", [(i, (i + 1) % bands) for i in range(bands)])
    vectors = [row(v) for v in (group_of, gain_first, shift_first, bias_first, gain_second, shift_second, bias_second)]
    outs = [parts_out, (latent.shape, BF16), pltpu.SMEM((8,), jnp.int32), ((1, channels), F32)]
    outs += [(v.shape, v.dtype) for v in vectors]
    scalars = pltpu.SMEM(clip_frames.shape, jnp.int32)
    parts, latent, plan, length, *vectors = call(
        stats_kernel, [HBM] * (3 + len(vectors)), outs,
        [scalars, scalars, pltpu.SemaphoreType.DMA((3 + len(vectors),))],
        cost=pl.CostEstimate(flops=1 << 32, bytes_accessed=1 << 24, transcendentals=0),
    )(*map(in_hbm, (clip_frames, clip_rank, latent, *vectors)))
    group_row = vectors[0]
    parts = gather(parts)
    hidden, parts = call(first_kernel, [SMEM] + [VMEM] * 9, [(latent.shape, BF16), parts_out], work)(
        in_smem(plan), length, parts, latent, above, *vectors[:4], taps(conv_first)
    )
    below = lax.ppermute(hidden, "space", [((i + 1) % bands, i) for i in range(bands)])
    parts = gather(parts)
    half = ((2, height, columns, channels), BF16)
    keep, send = call(second_kernel, [SMEM] + [VMEM] * 10, [half, half], work)(
        in_smem(plan), length, parts, hidden, below, latent, group_row, *vectors[4:], taps(conv_second),
    )
    got = lax.ppermute(send, "tm", [(i, i ^ 1) for i in range(clips)])
    chips = clips // 2
    got = list(call(spread_kernel, [SMEM] + [VMEM] * 2, [half] * chips)(in_smem(plan), keep, got))
    for step in range(1, chips):
        along = [(i, (i + 2 * step) % clips) for i in range(clips)]
        got[step] = lax.ppermute(got[step], "tm", along)
    (out,) = call(pick_kernel, [SMEM] + [ANY] * chips, [half], [pltpu.SemaphoreType.DMA((2,))], HBM)(in_smem(plan), *got)
    return out


def solution(mesh):
    placed = (P("tm", "space", None, None), P(), P(), P(), P(), P(), P(), P(), P(), P(), P(), P())
    return jax.shard_map(
        local, mesh=mesh, in_specs=placed, out_specs=P("tm", "space", None, None), check_vma=False
    )
```

```python
import functools

import jax
import jax.numpy as jnp
from jax import lax
from jax.experimental import pallas as pl
from jax.experimental.pallas import tpu as pltpu
from jax.sharding import PartitionSpec as P

G = 32
LANES = 128
EPSILON = 1e-06
F32 = jnp.float32
BF16 = jnp.bfloat16
VMEM = pl.BlockSpec(memory_space=pltpu.VMEM)
SMEM = pl.BlockSpec(memory_space=pltpu.SMEM)
HBM = pl.BlockSpec(memory_space=pltpu.HBM)
ANY = pl.BlockSpec(memory_space=pl.ANY)
LIMIT = 20 * 1024 * 1024


def member_rows(group_row):
    rows = lax.broadcasted_iota(jnp.int32, (LANES, group_row.shape[1]), 0)
    return ((rows == group_row) | (rows - G == group_row)).astype(F32).astype(BF16)


def clip_start_of(frames_ref, rank_ref, clip):
    start = jnp.int32(0)
    for k in range(frames_ref.shape[0]):
        start = start + jnp.where(rank_ref[k] < rank_ref[clip], frames_ref[k], 0)
    return start


def in_thirds(row):
    first = row.astype(BF16)
    row = row - first.astype(F32)
    second = row.astype(BF16)
    return [first, second, (row - second.astype(F32)).astype(BF16)]


def dot_rows(rows, members, side):
    pieces = [piece for row in rows for piece in in_thirds(row)]
    pad = jnp.zeros((16 - len(pieces), pieces[0].shape[1]), BF16)
    left = jnp.concatenate(pieces + [pad], axis=0)
    product = lax.dot_general(left, members, (((1,), (side,)), ((), ())), preferred_element_type=F32)
    return [jnp.sum(product[3 * i : 3 * i + 3], axis=0, keepdims=True) for i in range(len(rows))]


def local_stats(field_ref, length_row, group_row):
    frames, height, columns, channels = field_ref.shape
    pixels = height * columns
    entries = length_row * float(pixels)
    live = [jnp.where(length_row > f, 1.0, 0.0) for f in range(frames)]
    members = member_rows(group_row)
    share = float(G) / channels

    def frame(f):
        return field_ref[f].astype(F32).reshape(pixels, channels)

    mean = jnp.zeros((1, channels), F32)
    for f in range(frames):
        mean = mean + live[f] * jnp.sum(frame(f), axis=0, keepdims=True)
    mean = mean * (1.0 / entries)
    (group_mean,) = dot_rows([mean], members, 1)
    group_mean = group_mean * share
    lane = lax.broadcasted_iota(jnp.int32, (1, LANES), 1)
    group_mean = jnp.where(lane < G, group_mean, 0.0)
    (mean_back,) = dot_rows([group_mean], members, 0)
    spread = jnp.zeros((1, channels), F32)
    for f in range(frames):
        centred = frame(f) - mean
        spread = spread + live[f] * jnp.sum(centred * centred, axis=0, keepdims=True)
    away = mean - mean_back
    (group_spread,) = dot_rows([spread + away * away * entries], members, 1)
    return jnp.where(lane < G, group_mean, group_spread)


def combine_stats(parts, length_row, pixels, group_row):
    bands = parts.shape[0]
    channels = group_row.shape[1]
    per_band = length_row * float(pixels * (channels // G))
    lane = lax.broadcasted_iota(jnp.int32, (1, LANES), 1)
    sums = jnp.sum(parts, axis=0, keepdims=True)
    mean = sums * (1.0 / bands)
    away = parts - mean
    between = jnp.sum(away * away, axis=0, keepdims=True) * per_band[:, :LANES]
    spread = jnp.where(lane < G, between, jnp.where(lane < 2 * G, sums, 0.0))
    mean = jnp.where(lane < G, mean, 0.0)
    mean_back, spread_back = dot_rows([mean, spread], member_rows(group_row), 0)
    return mean_back, lax.rsqrt(spread_back / (per_band * bands) + EPSILON)


def activate(value, act_ref, slope, offset, place):
    channels = slope.shape[1]
    half = value.astype(F32) * slope + offset
    act = half * jnp.tanh(half) + half
    left = jnp.concatenate([act[:1], act[:-1]], axis=0)
    right = jnp.concatenate([act[1:], act[-1:]], axis=0)
    for step, taken in enumerate((left, act, right)):
        act_ref[place, :, step * channels : (step + 1) * channels] = taken.astype(BF16)


def convolve(own_ref, other_ref, own_first, act_refs, weight_ref, acc_refs, slope, offset, taken):
    frames = len(act_refs)
    height = own_ref.shape[1]
    width = act_refs[0].shape[2]
    own_place = jnp.where(own_first, 0, height)
    ready = 0
    for back_step, acc_ref in enumerate(acc_refs):
        used = frames - 2 + back_step
        for f in range(ready, used):
            for r in range(height):
                activate(own_ref[f, r], act_refs[f], slope, offset, own_place + r)
                activate(other_ref[f, r], act_refs[f], slope, offset, height - own_place + r)
        ready = used
        slabs = []
        for places in taken:
            pieces = [act_refs[f][place] for f in range(used) for place in places]
            slabs.append(jnp.concatenate(pieces, axis=0))
        kernel = weight_ref[3 * back_step : 3 * back_step + 3].reshape(3 * width, -1)
        part = jnp.dot(jnp.concatenate(slabs, axis=1), kernel, preferred_element_type=F32)
        acc_ref[...] = part.reshape(acc_ref.shape)


def frame_sum(acc_refs, f, zero):
    return acc_refs[0][max(f - 2, 0) + zero] + acc_refs[1][max(f - 1, 0) + zero] + acc_refs[2][f + zero]


def band_ends():
    band = lax.axis_index("space")
    return band == 0, band == lax.axis_size("space") - 1


def in_hbm(array):
    return pltpu.with_memory_space_constraint(array, pltpu.HBM)


def in_smem(array):
    return pltpu.with_memory_space_constraint(array, pltpu.SMEM)


def plan_of(frames_ref, rank_ref):
    count = frames_ref.shape[0]
    starts = [clip_start_of(frames_ref, rank_ref, k) for k in range(count)]
    clip = lax.axis_index("tm")
    core = lax.rem(clip, 2)
    other = clip + 1 - 2 * core
    chips = count // 2

    def entry(values, index):
        taken = jnp.int32(0)
        for k, value in enumerate(values):
            taken = taken + jnp.where(index == k, value, 0)
        return taken

    plan = [lax.rem(entry(starts, clip), 4), entry(starts, other), frames_ref[other]]
    for slot in range(2):
        place = 2 * clip + slot
        source = jnp.int32(0)
        for k, start in enumerate(starts):
            source = source + jnp.where((place >= start) & (place < start + frames_ref[k]), k // 2, 0)
        plan.append(lax.rem((1 - 2 * core) * (clip // 2 - source) + chips, chips))
    return plan


def stats_kernel(frames_hbm, rank_hbm, latent_hbm, *rest):
    rows = len(rest) // 2 - 3
    rows_hbm, rest = rest[:rows], rest[rows:]
    parts_ref, latent_ref, plan_ref, length_ref = rest[:4]
    rows_ref, (frames_ref, rank_ref, sem) = rest[4 : 4 + rows], rest[4 + rows :]
    group_ref = rows_ref[0]
    pairs = [(frames_hbm, frames_ref), (rank_hbm, rank_ref), (latent_hbm, latent_ref)] + list(zip(rows_hbm, rows_ref))
    copies = [pltpu.make_async_copy(source, target, sem.at[i]) for i, (source, target) in enumerate(pairs)]
    for copy in copies:
        copy.start()
    for copy in copies[:4]:
        copy.wait()
    length = frames_ref[lax.axis_index("tm")].astype(F32)
    length_row = jnp.full(length_ref.shape, length, F32)
    length_ref[...] = length_row
    row = local_stats(latent_ref, length_row, group_ref[...])
    parts_ref[...] = jnp.broadcast_to(row[None], parts_ref.shape)
    for k, value in enumerate(plan_of(frames_ref, rank_ref)):
        plan_ref[k] = value
    for copy in copies[4:]:
        copy.wait()


def first_kernel(
    plan_ref, length_ref, parts_ref, field_ref, other_ref, group_ref, gain_ref, shift_ref, bias_ref, weight_ref,
    hidden_ref, out_parts_ref,
    *work_refs,
):
    frames, height, columns, channels = field_ref.shape
    zero = jnp.minimum(plan_ref[0], 0)
    core = lax.rem(lax.axis_index("tm"), 2)
    top, bottom = band_ends()
    ends = jnp.where(core == 0, top, bottom)
    taken = [(0, jnp.where(ends, 2, 1)), (1, 2), (jnp.where(ends, 1, 2), 3)]
    mean, inverse = combine_stats(parts_ref[:, 0], length_ref[...], height * columns, group_ref[...])
    slope = inverse * gain_ref[...] * 0.5
    offset = shift_ref[...] * 0.5 - mean * slope
    act_refs, acc_refs = work_refs[:frames], work_refs[frames:]
    convolve(field_ref, other_ref, core == 1, act_refs, weight_ref, acc_refs, slope, offset, taken)
    for f in range(frames):
        hidden_ref[f] = (frame_sum(acc_refs, f, zero) + bias_ref[...]).astype(BF16)
    row = local_stats(hidden_ref, length_ref[...], group_ref[...])
    out_parts_ref[...] = jnp.broadcast_to(row[None], out_parts_ref.shape)


def second_kernel(
    plan_ref, length_ref, parts_ref, hidden_ref, other_ref, latent_ref, group_ref, gain_ref, shift_ref, bias_ref,
    weight_ref,
    keep_ref, send_ref,
    *work_refs,
):
    frames, height, columns, channels = latent_ref.shape
    core = lax.rem(lax.axis_index("tm"), 2)
    zero = jnp.minimum(plan_ref[0], 0)
    top, bottom = band_ends()
    taken = [(jnp.where(top, 1, 0), 1), (1, 2), (2, jnp.where(bottom, 2, 3))]
    mean, inverse = combine_stats(parts_ref[:, 0], length_ref[...], height * columns, group_ref[...])
    slope = inverse * gain_ref[...] * 0.5
    offset = shift_ref[...] * 0.5 - mean * slope
    act_refs, acc_refs = work_refs[:frames], work_refs[frames:]
    convolve(hidden_ref, other_ref, core == 0, act_refs, weight_ref, acc_refs, slope, offset, taken)
    for f in range(frames):
        total = (latent_ref[f].astype(F32) + (frame_sum(acc_refs, f, zero) + bias_ref[...])).astype(BF16)
        place = lax.rem(plan_ref[0] + f, 4)
        slot = lax.rem(place, 2)
        stays = place // 2 == core

        @pl.when(stays)
        def _():
            keep_ref[slot] = total

        @pl.when(jnp.logical_not(stays))
        def _():
            send_ref[slot] = total


def spread_kernel(plan_ref, keep_ref, got_ref, *out_refs):
    clip = lax.axis_index("tm")
    core = lax.rem(clip, 2)
    chips = len(out_refs)
    start, length = plan_ref[1], plan_ref[2]
    for step, out_ref in enumerate(out_refs):
        chip = lax.rem(clip // 2 + chips + (1 - 2 * core) * step, chips)
        for slot in range(2):
            place = 4 * chip + 2 * core + slot - start
            theirs = (place >= 0) & (place < length)
            out_ref[slot] = jnp.where(theirs, got_ref[slot], keep_ref[slot])


def pick_kernel(plan_ref, *rest):
    *got_refs, out_hbm, sem = rest
    copies = []
    for slot in range(2):
        step = plan_ref[3 + slot]
        for k, got_ref in enumerate(got_refs):
            copy = pltpu.make_async_copy(got_ref.at[slot], out_hbm.at[slot], sem.at[slot])
            pl.when(step == k)(copy.start)
        copies.append(copy)
    for copy in copies:
        copy.wait()


def call(kernel, in_specs, outs, scratch=(), out_spec=VMEM, cost=None):
    return pl.pallas_call(
        kernel,
        in_specs=in_specs,
        out_specs=[out_spec if isinstance(out, tuple) else SMEM for out in outs],
        out_shape=[jax.ShapeDtypeStruct(*out) if isinstance(out, tuple) else out for out in outs],
        scratch_shapes=list(scratch),
        compiler_params=pltpu.CompilerParams(vmem_limit_bytes=LIMIT),
        cost_estimate=cost,
    )


def local(
    latent,
    clip_frames,
    clip_rank,
    group_of,
    gain_first,
    shift_first,
    conv_first,
    bias_first,
    gain_second,
    shift_second,
    conv_second,
    bias_second,
):
    frames, height, columns, channels = latent.shape
    bands = lax.axis_size("space")
    clips = lax.axis_size("tm")
    row = lambda v: v.reshape(1, channels)
    taps = lambda k: k.reshape(9, 3 * channels, channels)
    group_row = row(group_of)
    parts_out = ((bands, 1, LANES), F32)

    def gather(parts):
        return lax.all_to_all(parts, "space", 0, 0, tiled=True)

    work = [pltpu.VMEM((4, columns, 3 * channels), BF16)] * frames
    work += [pltpu.VMEM((frames - 2 + i, height, columns, channels), F32) for i in range(3)]


    def from_neighbour(field, step):
        pairs = [
            (clip * bands + i, clip * bands + (i + (step if clip % 2 == 0 else -step)) % bands)
            for clip in range(clips)
            for i in range(bands)
        ]
        return lax.ppermute(field, ("tm", "space"), pairs)

    other = from_neighbour(latent, 1)
    vectors = [row(v) for v in (group_of, gain_first, shift_first, bias_first, gain_second, shift_second, bias_second)]
    outs = [parts_out, (latent.shape, BF16), pltpu.SMEM((8,), jnp.int32), ((1, channels), F32)]
    outs += [(v.shape, v.dtype) for v in vectors]
    scalars = pltpu.SMEM(clip_frames.shape, jnp.int32)
    parts, latent, plan, length, *vectors = call(
        stats_kernel, [HBM] * (3 + len(vectors)), outs,
        [scalars, scalars, pltpu.SemaphoreType.DMA((3 + len(vectors),))],
        cost=pl.CostEstimate(flops=1 << 32, bytes_accessed=1 << 24, transcendentals=0),
    )(*map(in_hbm, (clip_frames, clip_rank, latent, *vectors)))
    group_row = vectors[0]
    parts = gather(parts)
    hidden, parts = call(first_kernel, [SMEM] + [VMEM] * 9, [(latent.shape, BF16), parts_out], work)(
        in_smem(plan), length, parts, latent, other, *vectors[:4], taps(conv_first)
    )
    hidden_other = from_neighbour(hidden, -1)
    parts = gather(parts)
    half = ((2, height, columns, channels), BF16)
    keep, send = call(second_kernel, [SMEM] + [VMEM] * 10, [half, half], work)(
        in_smem(plan), length, parts, hidden, hidden_other, latent, group_row, *vectors[4:], taps(conv_second),
    )
    got = lax.ppermute(send, "tm", [(i, i ^ 1) for i in range(clips)])
    chips = clips // 2
    got = list(call(spread_kernel, [SMEM] + [VMEM] * 2, [half] * chips)(in_smem(plan), keep, got))
    for step in range(1, chips):
        along = [(i, (i + (2 * step if i % 2 == 0 else -2 * step)) % clips) for i in range(clips)]
        got[step] = lax.ppermute(got[step], "tm", along)
    (out,) = call(pick_kernel, [SMEM] + [ANY] * chips, [half], [pltpu.SemaphoreType.DMA((2,))], HBM)(in_smem(plan), *got)
    return out


def solution(mesh):
    placed = (P("tm", "space", None, None), P(), P(), P(), P(), P(), P(), P(), P(), P(), P(), P())
    return jax.shard_map(
        local, mesh=mesh, in_specs=placed, out_specs=P("tm", "space", None, None), check_vma=False
    )
```

```python
import functools

import jax
import jax.numpy as jnp
from jax import lax
from jax.experimental import pallas as pl
from jax.experimental.pallas import tpu as pltpu
from jax.sharding import PartitionSpec as P

G = 32
LANES = 128
EPSILON = 1e-06
F32 = jnp.float32
BF16 = jnp.bfloat16
VMEM = pl.BlockSpec(memory_space=pltpu.VMEM)
SMEM = pl.BlockSpec(memory_space=pltpu.SMEM)
HBM = pl.BlockSpec(memory_space=pltpu.HBM)
ANY = pl.BlockSpec(memory_space=pl.ANY)
LIMIT = 20 * 1024 * 1024


def member_rows(group_row):
    rows = lax.broadcasted_iota(jnp.int32, (LANES, group_row.shape[1]), 0)
    return ((rows == group_row) | (rows - G == group_row)).astype(F32).astype(BF16)


def clip_start_of(frames_ref, rank_ref, clip):
    start = jnp.int32(0)
    for k in range(frames_ref.shape[0]):
        start = start + jnp.where(rank_ref[k] < rank_ref[clip], frames_ref[k], 0)
    return start


def in_thirds(row):
    first = row.astype(BF16)
    row = row - first.astype(F32)
    second = row.astype(BF16)
    return [first, second, (row - second.astype(F32)).astype(BF16)]


def dot_rows(rows, members, side):
    pieces = [piece for row in rows for piece in in_thirds(row)]
    pad = jnp.zeros((16 - len(pieces), pieces[0].shape[1]), BF16)
    left = jnp.concatenate(pieces + [pad], axis=0)
    product = lax.dot_general(left, members, (((1,), (side,)), ((), ())), preferred_element_type=F32)
    return [jnp.sum(product[3 * i : 3 * i + 3], axis=0, keepdims=True) for i in range(len(rows))]


def local_stats(field_ref, length_row, group_row):
    frames, height, columns, channels = field_ref.shape
    pixels = height * columns
    entries = length_row * float(pixels)
    live = [jnp.where(length_row > f, 1.0, 0.0) for f in range(frames)]
    members = member_rows(group_row)
    share = float(G) / channels

    def frame(f):
        return field_ref[f].astype(F32).reshape(pixels, channels)

    mean = jnp.zeros((1, channels), F32)
    for f in range(frames):
        mean = mean + live[f] * jnp.sum(frame(f), axis=0, keepdims=True)
    mean = mean * (1.0 / entries)
    (group_mean,) = dot_rows([mean], members, 1)
    group_mean = group_mean * share
    lane = lax.broadcasted_iota(jnp.int32, (1, LANES), 1)
    group_mean = jnp.where(lane < G, group_mean, 0.0)
    (mean_back,) = dot_rows([group_mean], members, 0)
    spread = jnp.zeros((1, channels), F32)
    for f in range(frames):
        centred = frame(f) - mean
        spread = spread + live[f] * jnp.sum(centred * centred, axis=0, keepdims=True)
    away = mean - mean_back
    (group_spread,) = dot_rows([spread + away * away * entries], members, 1)
    return jnp.where(lane < G, group_mean, group_spread)


def combine_stats(parts, length_row, pixels, group_row):
    bands = parts.shape[0]
    channels = group_row.shape[1]
    per_band = length_row * float(pixels * (channels // G))
    lane = lax.broadcasted_iota(jnp.int32, (1, LANES), 1)
    sums = jnp.sum(parts, axis=0, keepdims=True)
    mean = sums * (1.0 / bands)
    away = parts - mean
    between = jnp.sum(away * away, axis=0, keepdims=True) * per_band[:, :LANES]
    spread = jnp.where(lane < G, between, jnp.where(lane < 2 * G, sums, 0.0))
    mean = jnp.where(lane < G, mean, 0.0)
    mean_back, spread_back = dot_rows([mean, spread], member_rows(group_row), 0)
    return mean_back, lax.rsqrt(spread_back / (per_band * bands) + EPSILON)


def activate(rows, act_ref, slope, offset, f):
    channels = slope.shape[1]
    for r in range(act_ref.shape[0]):
        half = rows(f, r).astype(F32) * slope + offset
        act = half * jnp.tanh(half) + half
        left = jnp.concatenate([act[:1], act[:-1]], axis=0)
        right = jnp.concatenate([act[1:], act[-1:]], axis=0)
        for step, taken in enumerate((left, act, right)):
            act_ref[r, :, step * channels : (step + 1) * channels] = taken.astype(BF16)


def convolve(rows, act_refs, weight_ref, acc_refs, slope, offset, taken):
    frames = len(act_refs)
    _, columns, width = act_refs[0].shape
    ready = 0
    for back_step, acc_ref in enumerate(acc_refs):
        used = frames - 2 + back_step
        for f in range(ready, used):
            activate(rows, act_refs[f], slope, offset, f)
        ready = used
        slabs = []
        for places in taken:
            pieces = [act_refs[f][place] for f in range(used) for place in places]
            slabs.append(jnp.concatenate(pieces, axis=0))
        kernel = weight_ref[3 * back_step : 3 * back_step + 3].reshape(3 * width, -1)
        part = jnp.dot(jnp.concatenate(slabs, axis=1), kernel, preferred_element_type=F32)
        acc_ref[...] = part.reshape(acc_ref.shape)


def frame_sum(acc_refs, f, zero):
    return acc_refs[0][max(f - 2, 0) + zero] + acc_refs[1][max(f - 1, 0) + zero] + acc_refs[2][f + zero]


def band_ends():
    band = lax.axis_index("space")
    return band == 0, band == lax.axis_size("space") - 1


def in_hbm(array):
    return pltpu.with_memory_space_constraint(array, pltpu.HBM)


def in_smem(array):
    return pltpu.with_memory_space_constraint(array, pltpu.SMEM)


def plan_of(frames_ref, rank_ref):
    count = frames_ref.shape[0]
    starts = [clip_start_of(frames_ref, rank_ref, k) for k in range(count)]
    clip = lax.axis_index("tm")
    core = lax.rem(clip, 2)
    other = clip + 1 - 2 * core
    chips = count // 2

    def entry(values, index):
        taken = jnp.int32(0)
        for k, value in enumerate(values):
            taken = taken + jnp.where(index == k, value, 0)
        return taken

    plan = [lax.rem(entry(starts, clip), 4), entry(starts, other), frames_ref[other]]
    for slot in range(2):
        place = 2 * clip + slot
        source = jnp.int32(0)
        for k, start in enumerate(starts):
            source = source + jnp.where((place >= start) & (place < start + frames_ref[k]), k // 2, 0)
        plan.append(lax.rem(clip // 2 - source + chips, chips))
    return plan


def stats_kernel(frames_hbm, rank_hbm, latent_hbm, *rest):
    rows = len(rest) // 2 - 3
    rows_hbm, rest = rest[:rows], rest[rows:]
    parts_ref, latent_ref, plan_ref, length_ref = rest[:4]
    rows_ref, (frames_ref, rank_ref, sem) = rest[4 : 4 + rows], rest[4 + rows :]
    group_ref = rows_ref[0]
    pairs = [(frames_hbm, frames_ref), (rank_hbm, rank_ref), (latent_hbm, latent_ref)] + list(zip(rows_hbm, rows_ref))
    copies = [pltpu.make_async_copy(source, target, sem.at[i]) for i, (source, target) in enumerate(pairs)]
    for copy in copies:
        copy.start()
    for copy in copies[:4]:
        copy.wait()
    length = frames_ref[lax.axis_index("tm")].astype(F32)
    length_row = jnp.full(length_ref.shape, length, F32)
    length_ref[...] = length_row
    row = local_stats(latent_ref, length_row, group_ref[...])
    parts_ref[...] = jnp.broadcast_to(row[None], parts_ref.shape)
    for k, value in enumerate(plan_of(frames_ref, rank_ref)):
        plan_ref[k] = value
    for copy in copies[4:]:
        copy.wait()


def first_kernel(
    plan_ref, length_ref, parts_ref, field_ref, above_ref, group_ref, gain_ref, shift_ref, bias_ref, weight_ref,
    hidden_ref, out_parts_ref,
    *work_refs,
):
    frames, height, columns, channels = field_ref.shape
    zero = jnp.minimum(plan_ref[0], 0)
    top, _ = band_ends()
    taken = [(0, jnp.where(top, 2, 1)), (1, 2), (jnp.where(top, 1, 2), 3)]
    mean, inverse = combine_stats(parts_ref[:, 0], length_ref[...], height * columns, group_ref[...])
    slope = inverse * gain_ref[...] * 0.5
    offset = shift_ref[...] * 0.5 - mean * slope

    def rows(f, r):
        return above_ref[f, r] if r < 2 else field_ref[f, r - 2]

    act_refs, acc_refs = work_refs[:frames], work_refs[frames:]
    convolve(rows, act_refs, weight_ref, acc_refs, slope, offset, taken)
    for f in range(frames):
        hidden_ref[f] = (frame_sum(acc_refs, f, zero) + bias_ref[...]).astype(BF16)
    row = local_stats(hidden_ref, length_ref[...], group_ref[...])
    out_parts_ref[...] = jnp.broadcast_to(row[None], out_parts_ref.shape)


def second_kernel(
    plan_ref, length_ref, parts_ref, hidden_ref, below_ref, latent_ref, group_ref, gain_ref, shift_ref, bias_ref,
    weight_ref,
    keep_ref, send_ref,
    *work_refs,
):
    frames, height, columns, channels = latent_ref.shape
    core = lax.rem(lax.axis_index("tm"), 2)
    zero = jnp.minimum(plan_ref[0], 0)
    top, bottom = band_ends()
    taken = [(jnp.where(top, 1, 0), 1), (1, 2), (2, jnp.where(bottom, 2, 3))]
    mean, inverse = combine_stats(parts_ref[:, 0], length_ref[...], height * columns, group_ref[...])
    slope = inverse * gain_ref[...] * 0.5
    offset = shift_ref[...] * 0.5 - mean * slope

    def rows(f, r):
        return hidden_ref[f, r] if r < 2 else below_ref[f, r - 2]

    act_refs, acc_refs = work_refs[:frames], work_refs[frames:]
    convolve(rows, act_refs, weight_ref, acc_refs, slope, offset, taken)
    for f in range(frames):
        total = (latent_ref[f].astype(F32) + (frame_sum(acc_refs, f, zero) + bias_ref[...])).astype(BF16)
        place = lax.rem(plan_ref[0] + f, 4)
        slot = lax.rem(place, 2)
        stays = place // 2 == core

        @pl.when(stays)
        def _():
            keep_ref[slot] = total

        @pl.when(jnp.logical_not(stays))
        def _():
            send_ref[slot] = total


def spread_kernel(plan_ref, keep_ref, got_ref, *out_refs):
    clip = lax.axis_index("tm")
    core = lax.rem(clip, 2)
    chips = len(out_refs)
    start, length = plan_ref[1], plan_ref[2]
    for step, out_ref in enumerate(out_refs):
        chip = lax.rem(clip // 2 + step, chips)
        for slot in range(2):
            place = 4 * chip + 2 * core + slot - start
            theirs = (place >= 0) & (place < length)
            out_ref[slot] = jnp.where(theirs, got_ref[slot], keep_ref[slot])


def pick_kernel(plan_ref, *rest):
    *got_refs, out_hbm, sem = rest
    copies = []
    for slot in range(2):
        step = plan_ref[3 + slot]
        for k, got_ref in enumerate(got_refs):
            copy = pltpu.make_async_copy(got_ref.at[slot], out_hbm.at[slot], sem.at[slot])
            pl.when(step == k)(copy.start)
        copies.append(copy)
    for copy in copies:
        copy.wait()


def call(kernel, in_specs, outs, scratch=(), out_spec=VMEM, cost=None):
    return pl.pallas_call(
        kernel,
        in_specs=in_specs,
        out_specs=[out_spec if isinstance(out, tuple) else SMEM for out in outs],
        out_shape=[jax.ShapeDtypeStruct(*out) if isinstance(out, tuple) else out for out in outs],
        scratch_shapes=list(scratch),
        compiler_params=pltpu.CompilerParams(vmem_limit_bytes=LIMIT),
        cost_estimate=cost,
    )


def local(
    latent,
    clip_frames,
    clip_rank,
    group_of,
    gain_first,
    shift_first,
    conv_first,
    bias_first,
    gain_second,
    shift_second,
    conv_second,
    bias_second,
):
    frames, height, columns, channels = latent.shape
    bands = lax.axis_size("space")
    clips = lax.axis_size("tm")
    row = lambda v: v.reshape(1, channels)
    taps = lambda k: k.reshape(9, 3 * channels, channels)
    group_row = row(group_of)
    parts_out = ((bands, 1, LANES), F32)

    def gather(parts, leader):
        order = [(leader + i) % bands for i in range(bands)]
        return lax.all_to_all(parts, "space", 0, 0, axis_index_groups=[order], tiled=True)

    work = [pltpu.VMEM((4, columns, 3 * channels), BF16)] * frames
    work += [pltpu.VMEM((frames - 2 + i, height, columns, channels), F32) for i in range(3)]

    above = lax.ppermute(latent, "space", [(i, (i + 1) % bands) for i in range(bands)])
    vectors = [row(v) for v in (group_of, gain_first, shift_first, bias_first, gain_second, shift_second, bias_second)]
    outs = [parts_out, (latent.shape, BF16), pltpu.SMEM((8,), jnp.int32), ((1, channels), F32)]
    outs += [(v.shape, v.dtype) for v in vectors]
    scalars = pltpu.SMEM(clip_frames.shape, jnp.int32)
    parts, latent, plan, length, *vectors = call(
        stats_kernel, [HBM] * (3 + len(vectors)), outs,
        [scalars, scalars, pltpu.SemaphoreType.DMA((3 + len(vectors),))],
        cost=pl.CostEstimate(flops=1 << 32, bytes_accessed=1 << 24, transcendentals=0),
    )(*map(in_hbm, (clip_frames, clip_rank, latent, *vectors)))
    group_row = vectors[0]
    parts = gather(parts, 3 * bands // 8)
    hidden, parts = call(first_kernel, [SMEM] + [VMEM] * 9, [(latent.shape, BF16), parts_out], work)(
        in_smem(plan), length, parts, latent, above, *vectors[:4], taps(conv_first)
    )
    below = lax.ppermute(hidden, "space", [((i + 1) % bands, i) for i in range(bands)])
    parts = gather(parts, 5 * bands // 8)
    half = ((2, height, columns, channels), BF16)
    keep, send = call(second_kernel, [SMEM] + [VMEM] * 10, [half, half], work)(
        in_smem(plan), length, parts, hidden, below, latent, group_row, *vectors[4:], taps(conv_second),
    )
    got = lax.ppermute(send, "tm", [(i, i ^ 1) for i in range(clips)])
    chips = clips // 2
    got = list(call(spread_kernel, [SMEM] + [VMEM] * 2, [half] * chips)(in_smem(plan), keep, got))
    for step in range(1, chips):
        along = [(i, (i + 2 * step) % clips) for i in range(clips)]
        got[step] = lax.ppermute(got[step], "tm", along)
    (out,) = call(pick_kernel, [SMEM] + [ANY] * chips, [half], [pltpu.SemaphoreType.DMA((2,))], HBM)(in_smem(plan), *got)
    return out


def solution(mesh):
    placed = (P("tm", "space", None, None), P(), P(), P(), P(), P(), P(), P(), P(), P(), P(), P())
    return jax.shard_map(
        local, mesh=mesh, in_specs=placed, out_specs=P("tm", "space", None, None), check_vma=False
    )
```

```python
import functools

import jax
import jax.numpy as jnp
from jax import lax
from jax.experimental import pallas as pl
from jax.experimental.pallas import tpu as pltpu
from jax.sharding import PartitionSpec as P

G = 32
LANES = 128
EPSILON = 1e-06
F32 = jnp.float32
BF16 = jnp.bfloat16
VMEM = pl.BlockSpec(memory_space=pltpu.VMEM)
SMEM = pl.BlockSpec(memory_space=pltpu.SMEM)
HBM = pl.BlockSpec(memory_space=pltpu.HBM)
ANY = pl.BlockSpec(memory_space=pl.ANY)
LIMIT = 20 * 1024 * 1024


def member_rows(group_row):
    rows = lax.broadcasted_iota(jnp.int32, (LANES, group_row.shape[1]), 0)
    return ((rows == group_row) | (rows - G == group_row)).astype(F32).astype(BF16)


def clip_start_of(frames_ref, rank_ref, clip):
    start = jnp.int32(0)
    for k in range(frames_ref.shape[0]):
        start = start + jnp.where(rank_ref[k] < rank_ref[clip], frames_ref[k], 0)
    return start


def in_thirds(row):
    first = row.astype(BF16)
    row = row - first.astype(F32)
    second = row.astype(BF16)
    return [first, second, (row - second.astype(F32)).astype(BF16)]


def dot_rows(rows, members, side):
    pieces = [piece for row in rows for piece in in_thirds(row)]
    pad = jnp.zeros((16 - len(pieces), pieces[0].shape[1]), BF16)
    left = jnp.concatenate(pieces + [pad], axis=0)
    product = lax.dot_general(left, members, (((1,), (side,)), ((), ())), preferred_element_type=F32)
    return [jnp.sum(product[3 * i : 3 * i + 3], axis=0, keepdims=True) for i in range(len(rows))]


def local_stats(field_ref, length_row, group_row):
    frames, height, columns, channels = field_ref.shape
    pixels = height * columns
    entries = length_row * float(pixels)
    live = [jnp.where(length_row > f, 1.0, 0.0) for f in range(frames)]
    members = member_rows(group_row)
    share = float(G) / channels

    def frame(f):
        return field_ref[f].astype(F32).reshape(pixels, channels)

    mean = jnp.zeros((1, channels), F32)
    for f in range(frames):
        mean = mean + live[f] * jnp.sum(frame(f), axis=0, keepdims=True)
    mean = mean * (1.0 / entries)
    (group_mean,) = dot_rows([mean], members, 1)
    group_mean = group_mean * share
    lane = lax.broadcasted_iota(jnp.int32, (1, LANES), 1)
    group_mean = jnp.where(lane < G, group_mean, 0.0)
    (mean_back,) = dot_rows([group_mean], members, 0)
    spread = jnp.zeros((1, channels), F32)
    for f in range(frames):
        centred = frame(f) - mean
        spread = spread + live[f] * jnp.sum(centred * centred, axis=0, keepdims=True)
    away = mean - mean_back
    (group_spread,) = dot_rows([spread + away * away * entries], members, 1)
    return jnp.where(lane < G, group_mean, group_spread)


def combine_stats(parts, length_row, pixels, group_row):
    bands = parts.shape[0]
    channels = group_row.shape[1]
    per_band = length_row * float(pixels * (channels // G))
    lane = lax.broadcasted_iota(jnp.int32, (1, LANES), 1)
    sums = jnp.sum(parts, axis=0, keepdims=True)
    mean = sums * (1.0 / bands)
    away = parts - mean
    between = jnp.sum(away * away, axis=0, keepdims=True) * per_band[:, :LANES]
    spread = jnp.where(lane < G, between, jnp.where(lane < 2 * G, sums, 0.0))
    mean = jnp.where(lane < G, mean, 0.0)
    mean_back, spread_back = dot_rows([mean, spread], member_rows(group_row), 0)
    return mean_back, lax.rsqrt(spread_back / (per_band * bands) + EPSILON)


def activate(rows, act_ref, slope, offset, f):
    channels = slope.shape[1]
    for r in range(act_ref.shape[0]):
        half = rows(f, r).astype(F32) * slope + offset
        act = half * jnp.tanh(half) + half
        left = jnp.concatenate([act[:1], act[:-1]], axis=0)
        right = jnp.concatenate([act[1:], act[-1:]], axis=0)
        for step, taken in enumerate((left, act, right)):
            act_ref[r, :, step * channels : (step + 1) * channels] = taken.astype(BF16)


def convolve(rows, act_refs, weight_ref, acc_refs, slope, offset, taken):
    frames = len(act_refs)
    _, columns, width = act_refs[0].shape
    ready = 0
    for back_step, acc_ref in enumerate(acc_refs):
        used = frames - 2 + back_step
        for f in range(ready, used):
            activate(rows, act_refs[f], slope, offset, f)
        ready = used
        slabs = []
        for places in taken:
            pieces = [act_refs[f][place] for f in range(used) for place in places]
            slabs.append(jnp.concatenate(pieces, axis=0))
        kernel = weight_ref[3 * back_step : 3 * back_step + 3].reshape(3 * width, -1)
        part = jnp.dot(jnp.concatenate(slabs, axis=1), kernel, preferred_element_type=F32)
        acc_ref[...] = part.reshape(acc_ref.shape)


def frame_sum(acc_refs, f, zero):
    return acc_refs[0][max(f - 2, 0) + zero] + acc_refs[1][max(f - 1, 0) + zero] + acc_refs[2][f + zero]


def band_ends():
    band = lax.axis_index("space")
    return band == 0, band == lax.axis_size("space") - 1


def in_hbm(array):
    return pltpu.with_memory_space_constraint(array, pltpu.HBM)


def in_smem(array):
    return pltpu.with_memory_space_constraint(array, pltpu.SMEM)


def plan_of(frames_ref, rank_ref):
    count = frames_ref.shape[0]
    starts = [clip_start_of(frames_ref, rank_ref, k) for k in range(count)]
    clip = lax.axis_index("tm")
    core = lax.rem(clip, 2)
    other = clip + 1 - 2 * core
    chips = count // 2

    def entry(values, index):
        taken = jnp.int32(0)
        for k, value in enumerate(values):
            taken = taken + jnp.where(index == k, value, 0)
        return taken

    plan = [lax.rem(entry(starts, clip), 4), entry(starts, other), frames_ref[other]]
    for slot in range(2):
        place = 2 * clip + slot
        source = jnp.int32(0)
        for k, start in enumerate(starts):
            source = source + jnp.where((place >= start) & (place < start + frames_ref[k]), k // 2, 0)
        plan.append(lax.rem(clip // 2 - source + chips, chips))
    return plan


def stats_kernel(frames_hbm, rank_hbm, latent_hbm, *rest):
    rows = len(rest) // 2 - 3
    rows_hbm, rest = rest[:rows], rest[rows:]
    parts_ref, latent_ref, plan_ref, length_ref = rest[:4]
    rows_ref, (frames_ref, rank_ref, sem) = rest[4 : 4 + rows], rest[4 + rows :]
    group_ref = rows_ref[0]
    pairs = [(frames_hbm, frames_ref), (rank_hbm, rank_ref), (latent_hbm, latent_ref)] + list(zip(rows_hbm, rows_ref))
    copies = [pltpu.make_async_copy(source, target, sem.at[i]) for i, (source, target) in enumerate(pairs)]
    for copy in copies:
        copy.start()
    for copy in copies[:4]:
        copy.wait()
    length = frames_ref[lax.axis_index("tm")].astype(F32)
    length_row = jnp.full(length_ref.shape, length, F32)
    length_ref[...] = length_row
    row = local_stats(latent_ref, length_row, group_ref[...])
    parts_ref[...] = jnp.broadcast_to(row[None], parts_ref.shape)
    for k, value in enumerate(plan_of(frames_ref, rank_ref)):
        plan_ref[k] = value
    for copy in copies[4:]:
        copy.wait()


def first_kernel(
    plan_ref, length_ref, parts_ref, field_ref, above_ref, group_ref, gain_ref, shift_ref, bias_ref, weight_ref,
    hidden_ref, out_parts_ref,
    *work_refs,
):
    frames, height, columns, channels = field_ref.shape
    zero = jnp.minimum(plan_ref[0], 0)
    top, _ = band_ends()
    taken = [(0, jnp.where(top, 2, 1)), (1, 2), (jnp.where(top, 1, 2), 3)]
    mean, inverse = combine_stats(parts_ref[:, 0], length_ref[...], height * columns, group_ref[...])
    slope = inverse * gain_ref[...] * 0.5
    offset = shift_ref[...] * 0.5 - mean * slope

    def rows(f, r):
        return above_ref[f, r] if r < 2 else field_ref[f, r - 2]

    act_refs, acc_refs = work_refs[:frames], work_refs[frames:]
    convolve(rows, act_refs, weight_ref, acc_refs, slope, offset, taken)
    for f in range(frames):
        hidden_ref[f] = (frame_sum(acc_refs, f, zero) + bias_ref[...]).astype(BF16)
    row = local_stats(hidden_ref, length_ref[...], group_ref[...])
    out_parts_ref[...] = jnp.broadcast_to(row[None], out_parts_ref.shape)


def second_kernel(
    plan_ref, length_ref, parts_ref, hidden_ref, below_ref, latent_ref, group_ref, gain_ref, shift_ref, bias_ref,
    weight_ref,
    keep_ref, send_ref,
    *work_refs,
):
    frames, height, columns, channels = latent_ref.shape
    core = lax.rem(lax.axis_index("tm"), 2)
    zero = jnp.minimum(plan_ref[0], 0)
    top, bottom = band_ends()
    taken = [(jnp.where(top, 1, 0), 1), (1, 2), (2, jnp.where(bottom, 2, 3))]
    mean, inverse = combine_stats(parts_ref[:, 0], length_ref[...], height * columns, group_ref[...])
    slope = inverse * gain_ref[...] * 0.5
    offset = shift_ref[...] * 0.5 - mean * slope

    def rows(f, r):
        return hidden_ref[f, r] if r < 2 else below_ref[f, r - 2]

    act_refs, acc_refs = work_refs[:frames], work_refs[frames:]
    convolve(rows, act_refs, weight_ref, acc_refs, slope, offset, taken)
    for f in range(frames):
        total = (latent_ref[f].astype(F32) + (frame_sum(acc_refs, f, zero) + bias_ref[...])).astype(BF16)
        place = lax.rem(plan_ref[0] + f, 4)
        slot = lax.rem(place, 2)
        stays = place // 2 == core

        @pl.when(stays)
        def _():
            keep_ref[slot] = total

        @pl.when(jnp.logical_not(stays))
        def _():
            send_ref[slot] = total


def spread_kernel(plan_ref, keep_ref, got_ref, *out_refs):
    clip = lax.axis_index("tm")
    core = lax.rem(clip, 2)
    chips = len(out_refs)
    start, length = plan_ref[1], plan_ref[2]
    for step, out_ref in enumerate(out_refs):
        chip = lax.rem(clip // 2 + step, chips)
        for slot in range(2):
            place = 4 * chip + 2 * core + slot - start
            theirs = (place >= 0) & (place < length)
            out_ref[slot] = jnp.where(theirs, got_ref[slot], keep_ref[slot])


def pick_kernel(plan_ref, *rest):
    *got_refs, out_hbm, sem = rest
    copies = []
    for slot in range(2):
        step = plan_ref[3 + slot]
        for k, got_ref in enumerate(got_refs):
            copy = pltpu.make_async_copy(got_ref.at[slot], out_hbm.at[slot], sem.at[slot])
            pl.when(step == k)(copy.start)
        copies.append(copy)
    for copy in copies:
        copy.wait()


def call(kernel, in_specs, outs, scratch=(), out_spec=VMEM, cost=None):
    return pl.pallas_call(
        kernel,
        in_specs=in_specs,
        out_specs=[out_spec if isinstance(out, tuple) else SMEM for out in outs],
        out_shape=[jax.ShapeDtypeStruct(*out) if isinstance(out, tuple) else out for out in outs],
        scratch_shapes=list(scratch),
        compiler_params=pltpu.CompilerParams(vmem_limit_bytes=LIMIT),
        cost_estimate=cost,
    )


def local(
    latent,
    clip_frames,
    clip_rank,
    group_of,
    gain_first,
    shift_first,
    conv_first,
    bias_first,
    gain_second,
    shift_second,
    conv_second,
    bias_second,
):
    frames, height, columns, channels = latent.shape
    bands = lax.axis_size("space")
    clips = lax.axis_size("tm")
    row = lambda v: v.reshape(1, channels)
    taps = lambda k: k.reshape(9, 3 * channels, channels)
    group_row = row(group_of)
    parts_out = ((bands, 1, LANES), F32)

    def gather(parts, leader):
        order = [(leader + bands // 4 * i + i // 4) % bands for i in range(bands)]
        return lax.all_to_all(parts, "space", 0, 0, axis_index_groups=[order], tiled=True)

    work = [pltpu.VMEM((4, columns, 3 * channels), BF16)] * frames
    work += [pltpu.VMEM((frames - 2 + i, height, columns, channels), F32) for i in range(3)]

    above = lax.ppermute(latent, "space", [(i, (i + 1) % bands) for i in range(bands)])
    vectors = [row(v) for v in (group_of, gain_first, shift_first, bias_first, gain_second, shift_second, bias_second)]
    outs = [parts_out, (latent.shape, BF16), pltpu.SMEM((8,), jnp.int32), ((1, channels), F32)]
    outs += [(v.shape, v.dtype) for v in vectors]
    scalars = pltpu.SMEM(clip_frames.shape, jnp.int32)
    parts, latent, plan, length, *vectors = call(
        stats_kernel, [HBM] * (3 + len(vectors)), outs,
        [scalars, scalars, pltpu.SemaphoreType.DMA((3 + len(vectors),))],
        cost=pl.CostEstimate(flops=1 << 32, bytes_accessed=1 << 24, transcendentals=0),
    )(*map(in_hbm, (clip_frames, clip_rank, latent, *vectors)))
    group_row = vectors[0]
    parts = gather(parts, 3 * bands // 8 - 1)
    hidden, parts = call(first_kernel, [SMEM] + [VMEM] * 9, [(latent.shape, BF16), parts_out], work)(
        in_smem(plan), length, parts, latent, above, *vectors[:4], taps(conv_first)
    )
    below = lax.ppermute(hidden, "space", [((i + 1) % bands, i) for i in range(bands)])
    parts = gather(parts, 5 * bands // 8)
    half = ((2, height, columns, channels), BF16)
    keep, send = call(second_kernel, [SMEM] + [VMEM] * 10, [half, half], work)(
        in_smem(plan), length, parts, hidden, below, latent, group_row, *vectors[4:], taps(conv_second),
    )
    got = lax.ppermute(send, "tm", [(i, i ^ 1) for i in range(clips)])
    chips = clips // 2
    got = list(call(spread_kernel, [SMEM] + [VMEM] * 2, [half] * chips)(in_smem(plan), keep, got))
    for step in range(1, chips):
        along = [(i, (i + 2 * step) % clips) for i in range(clips)]
        got[step] = lax.ppermute(got[step], "tm", along)
    (out,) = call(pick_kernel, [SMEM] + [ANY] * chips, [half], [pltpu.SemaphoreType.DMA((2,))], HBM)(in_smem(plan), *got)
    return out


def solution(mesh):
    placed = (P("tm", "space", None, None), P(), P(), P(), P(), P(), P(), P(), P(), P(), P(), P())
    return jax.shard_map(
        local, mesh=mesh, in_specs=placed, out_specs=P("tm", "space", None, None), check_vma=False
    )
```

```python
import functools

import jax
import jax.numpy as jnp
from jax import lax
from jax.experimental import pallas as pl
from jax.experimental.pallas import tpu as pltpu
from jax.sharding import PartitionSpec as P

G = 32
LANES = 128
EPSILON = 1e-06
F32 = jnp.float32
BF16 = jnp.bfloat16
VMEM = pl.BlockSpec(memory_space=pltpu.VMEM)
SMEM = pl.BlockSpec(memory_space=pltpu.SMEM)
HBM = pl.BlockSpec(memory_space=pltpu.HBM)
ANY = pl.BlockSpec(memory_space=pl.ANY)
LIMIT = 20 * 1024 * 1024


def member_rows(group_row):
    rows = lax.broadcasted_iota(jnp.int32, (LANES, group_row.shape[1]), 0)
    return ((rows == group_row) | (rows - G == group_row)).astype(F32).astype(BF16)


def clip_start_of(frames_ref, rank_ref, clip):
    start = jnp.int32(0)
    for k in range(frames_ref.shape[0]):
        start = start + jnp.where(rank_ref[k] < rank_ref[clip], frames_ref[k], 0)
    return start


def in_thirds(row):
    first = row.astype(BF16)
    row = row - first.astype(F32)
    second = row.astype(BF16)
    return [first, second, (row - second.astype(F32)).astype(BF16)]


def dot_rows(rows, members, side):
    pieces = [piece for row in rows for piece in in_thirds(row)]
    pad = jnp.zeros((16 - len(pieces), pieces[0].shape[1]), BF16)
    left = jnp.concatenate(pieces + [pad], axis=0)
    product = lax.dot_general(left, members, (((1,), (side,)), ((), ())), preferred_element_type=F32)
    return [jnp.sum(product[3 * i : 3 * i + 3], axis=0, keepdims=True) for i in range(len(rows))]


def local_stats(field_ref, length_row, group_row):
    frames, height, columns, channels = field_ref.shape
    pixels = height * columns
    entries = length_row * float(pixels)
    live = [jnp.where(length_row > f, 1.0, 0.0) for f in range(frames)]
    members = member_rows(group_row)
    share = float(G) / channels

    def frame(f):
        return field_ref[f].astype(F32).reshape(pixels, channels)

    mean = jnp.zeros((1, channels), F32)
    for f in range(frames):
        mean = mean + live[f] * jnp.sum(frame(f), axis=0, keepdims=True)
    mean = mean * (1.0 / entries)
    (group_mean,) = dot_rows([mean], members, 1)
    group_mean = group_mean * share
    lane = lax.broadcasted_iota(jnp.int32, (1, LANES), 1)
    group_mean = jnp.where(lane < G, group_mean, 0.0)
    (mean_back,) = dot_rows([group_mean], members, 0)
    spread = jnp.zeros((1, channels), F32)
    for f in range(frames):
        centred = frame(f) - mean
        spread = spread + live[f] * jnp.sum(centred * centred, axis=0, keepdims=True)
    away = mean - mean_back
    (group_spread,) = dot_rows([spread + away * away * entries], members, 1)
    return jnp.where(lane < G, group_mean, group_spread)


def combine_stats(parts, length_row, pixels, group_row):
    bands = parts.shape[0]
    channels = group_row.shape[1]
    per_band = length_row * float(pixels * (channels // G))
    lane = lax.broadcasted_iota(jnp.int32, (1, LANES), 1)
    sums = jnp.sum(parts, axis=0, keepdims=True)
    mean = sums * (1.0 / bands)
    away = parts - mean
    between = jnp.sum(away * away, axis=0, keepdims=True) * per_band[:, :LANES]
    spread = jnp.where(lane < G, between, jnp.where(lane < 2 * G, sums, 0.0))
    mean = jnp.where(lane < G, mean, 0.0)
    mean_back, spread_back = dot_rows([mean, spread], member_rows(group_row), 0)
    return mean_back, lax.rsqrt(spread_back / (per_band * bands) + EPSILON)


def activate(rows, act_ref, slope, offset, f):
    channels = slope.shape[1]
    for r in range(act_ref.shape[0]):
        half = rows(f, r).astype(F32) * slope + offset
        act = half * jnp.tanh(half) + half
        left = jnp.concatenate([act[:1], act[:-1]], axis=0)
        right = jnp.concatenate([act[1:], act[-1:]], axis=0)
        for step, taken in enumerate((left, act, right)):
            act_ref[r, :, step * channels : (step + 1) * channels] = taken.astype(BF16)


def convolve(rows, act_refs, weight_ref, acc_refs, slope, offset, taken):
    frames = len(act_refs)
    _, columns, width = act_refs[0].shape
    ready = 0
    for back_step, acc_ref in enumerate(acc_refs):
        used = frames - 2 + back_step
        for f in range(ready, used):
            activate(rows, act_refs[f], slope, offset, f)
        ready = used
        slabs = []
        for places in taken:
            pieces = [act_refs[f][place] for f in range(used) for place in places]
            slabs.append(jnp.concatenate(pieces, axis=0))
        kernel = weight_ref[3 * back_step : 3 * back_step + 3].reshape(3 * width, -1)
        part = jnp.dot(jnp.concatenate(slabs, axis=1), kernel, preferred_element_type=F32)
        acc_ref[...] = part.reshape(acc_ref.shape)


def frame_sum(acc_refs, f, zero):
    return acc_refs[0][max(f - 2, 0) + zero] + acc_refs[1][max(f - 1, 0) + zero] + acc_refs[2][f + zero]


def band_ends():
    band = lax.axis_index("space")
    return band == 0, band == lax.axis_size("space") - 1


def in_hbm(array):
    return pltpu.with_memory_space_constraint(array, pltpu.HBM)


def in_smem(array):
    return pltpu.with_memory_space_constraint(array, pltpu.SMEM)


def plan_of(frames_ref, rank_ref):
    count = frames_ref.shape[0]
    starts = [clip_start_of(frames_ref, rank_ref, k) for k in range(count)]
    clip = lax.axis_index("tm")
    core = lax.rem(clip, 2)
    other = clip + 1 - 2 * core
    chips = count // 2

    def entry(values, index):
        taken = jnp.int32(0)
        for k, value in enumerate(values):
            taken = taken + jnp.where(index == k, value, 0)
        return taken

    plan = [lax.rem(entry(starts, clip), 4), entry(starts, other), frames_ref[other]]
    for slot in range(2):
        place = 2 * clip + slot
        source = jnp.int32(0)
        for k, start in enumerate(starts):
            source = source + jnp.where((place >= start) & (place < start + frames_ref[k]), k // 2, 0)
        plan.append(lax.rem(clip // 2 - source + chips, chips))
    return plan


def stats_kernel(frames_hbm, rank_hbm, latent_hbm, *rest):
    rows = len(rest) // 2 - 3
    rows_hbm, rest = rest[:rows], rest[rows:]
    parts_ref, latent_ref, plan_ref, length_ref = rest[:4]
    rows_ref, (frames_ref, rank_ref, sem) = rest[4 : 4 + rows], rest[4 + rows :]
    group_ref = rows_ref[0]
    pairs = [(latent_hbm, latent_ref), (frames_hbm, frames_ref), (rank_hbm, rank_ref)] + list(zip(rows_hbm, rows_ref))
    copies = [pltpu.make_async_copy(source, target, sem.at[i]) for i, (source, target) in enumerate(pairs)]
    for copy in copies:
        copy.start()
    for copy in copies[1:4]:
        copy.wait()
    copies[0].wait()
    length = frames_ref[lax.axis_index("tm")].astype(F32)
    length_row = jnp.full(length_ref.shape, length, F32)
    length_ref[...] = length_row
    row = local_stats(latent_ref, length_row, group_ref[...])
    parts_ref[...] = jnp.broadcast_to(row[None], parts_ref.shape)
    for k, value in enumerate(plan_of(frames_ref, rank_ref)):
        plan_ref[k] = value
    for copy in copies[4:]:
        copy.wait()


def first_kernel(
    plan_ref, length_ref, parts_ref, field_ref, above_ref, group_ref, gain_ref, shift_ref, bias_ref, weight_ref,
    hidden_ref, out_parts_ref,
    *work_refs,
):
    frames, height, columns, channels = field_ref.shape
    zero = jnp.minimum(plan_ref[0], 0)
    top, _ = band_ends()
    taken = [(0, jnp.where(top, 2, 1)), (1, 2), (jnp.where(top, 1, 2), 3)]
    mean, inverse = combine_stats(parts_ref[:, 0], length_ref[...], height * columns, group_ref[...])
    slope = inverse * gain_ref[...] * 0.5
    offset = shift_ref[...] * 0.5 - mean * slope

    def rows(f, r):
        return above_ref[f, r] if r < 2 else field_ref[f, r - 2]

    act_refs, acc_refs = work_refs[:frames], work_refs[frames:]
    convolve(rows, act_refs, weight_ref, acc_refs, slope, offset, taken)
    for f in range(frames):
        hidden_ref[f] = (frame_sum(acc_refs, f, zero) + bias_ref[...]).astype(BF16)
    row = local_stats(hidden_ref, length_ref[...], group_ref[...])
    out_parts_ref[...] = jnp.broadcast_to(row[None], out_parts_ref.shape)


def second_kernel(
    plan_ref, length_ref, parts_ref, hidden_ref, below_ref, latent_ref, group_ref, gain_ref, shift_ref, bias_ref,
    weight_ref,
    keep_ref, send_ref,
    *work_refs,
):
    frames, height, columns, channels = latent_ref.shape
    core = lax.rem(lax.axis_index("tm"), 2)
    zero = jnp.minimum(plan_ref[0], 0)
    top, bottom = band_ends()
    taken = [(jnp.where(top, 1, 0), 1), (1, 2), (2, jnp.where(bottom, 2, 3))]
    mean, inverse = combine_stats(parts_ref[:, 0], length_ref[...], height * columns, group_ref[...])
    slope = inverse * gain_ref[...] * 0.5
    offset = shift_ref[...] * 0.5 - mean * slope

    def rows(f, r):
        return hidden_ref[f, r] if r < 2 else below_ref[f, r - 2]

    act_refs, acc_refs = work_refs[:frames], work_refs[frames:]
    convolve(rows, act_refs, weight_ref, acc_refs, slope, offset, taken)
    for f in range(frames):
        total = (latent_ref[f].astype(F32) + (frame_sum(acc_refs, f, zero) + bias_ref[...])).astype(BF16)
        place = lax.rem(plan_ref[0] + f, 4)
        slot = lax.rem(place, 2)
        stays = place // 2 == core

        @pl.when(stays)
        def _():
            keep_ref[slot] = total

        @pl.when(jnp.logical_not(stays))
        def _():
            send_ref[slot] = total


def spread_kernel(plan_ref, keep_ref, got_ref, *out_refs):
    clip = lax.axis_index("tm")
    core = lax.rem(clip, 2)
    chips = len(out_refs)
    start, length = plan_ref[1], plan_ref[2]
    for step, out_ref in enumerate(out_refs):
        chip = lax.rem(clip // 2 + step, chips)
        for slot in range(2):
            place = 4 * chip + 2 * core + slot - start
            theirs = (place >= 0) & (place < length)
            out_ref[slot] = jnp.where(theirs, got_ref[slot], keep_ref[slot])


def pick_kernel(plan_ref, *rest):
    *got_refs, out_hbm, sem = rest
    copies = []
    for slot in range(2):
        step = plan_ref[3 + slot]
        for k, got_ref in enumerate(got_refs):
            copy = pltpu.make_async_copy(got_ref.at[slot], out_hbm.at[slot], sem.at[slot])
            pl.when(step == k)(copy.start)
        copies.append(copy)
    for copy in copies:
        copy.wait()


def call(kernel, in_specs, outs, scratch=(), out_spec=VMEM, cost=None):
    return pl.pallas_call(
        kernel,
        in_specs=in_specs,
        out_specs=[out_spec if isinstance(out, tuple) else SMEM for out in outs],
        out_shape=[jax.ShapeDtypeStruct(*out) if isinstance(out, tuple) else out for out in outs],
        scratch_shapes=list(scratch),
        compiler_params=pltpu.CompilerParams(vmem_limit_bytes=LIMIT),
        cost_estimate=cost,
    )


def local(
    latent,
    clip_frames,
    clip_rank,
    group_of,
    gain_first,
    shift_first,
    conv_first,
    bias_first,
    gain_second,
    shift_second,
    conv_second,
    bias_second,
):
    frames, height, columns, channels = latent.shape
    bands = lax.axis_size("space")
    clips = lax.axis_size("tm")
    row = lambda v: v.reshape(1, channels)
    taps = lambda k: k.reshape(9, 3 * channels, channels)
    group_row = row(group_of)
    parts_out = ((bands, 1, LANES), F32)

    def gather(parts, leaders):
        groups = [
            [clip * bands + (leaders[clip % 2] + bands // 4 * i + i // 4) % bands for i in range(bands)]
            for clip in range(clips)
        ]
        return lax.all_to_all(parts, ("tm", "space"), 0, 0, axis_index_groups=groups, tiled=True)

    work = [pltpu.VMEM((4, columns, 3 * channels), BF16)] * frames
    work += [pltpu.VMEM((frames - 2 + i, height, columns, channels), F32) for i in range(3)]

    vectors = [row(v) for v in (group_of, gain_first, shift_first, bias_first, gain_second, shift_second, bias_second)]
    outs = [parts_out, (latent.shape, BF16), pltpu.SMEM((8,), jnp.int32), ((1, channels), F32)]
    outs += [(v.shape, v.dtype) for v in vectors]
    scalars = pltpu.SMEM(clip_frames.shape, jnp.int32)
    parts, latent, plan, length, *vectors = call(
        stats_kernel, [HBM] * (3 + len(vectors)), outs,
        [scalars, scalars, pltpu.SemaphoreType.DMA((3 + len(vectors),))],
        cost=pl.CostEstimate(flops=1 << 32, bytes_accessed=1 << 24, transcendentals=0),
    )(*map(in_hbm, (clip_frames, clip_rank, latent, *vectors)))
    group_row = vectors[0]
    above = lax.ppermute(latent, "space", [(i, (i + 1) % bands) for i in range(bands)])
    parts = gather(parts, (11, 20))
    hidden, parts = call(first_kernel, [SMEM] + [VMEM] * 9, [(latent.shape, BF16), parts_out], work)(
        in_smem(plan), length, parts, latent, above, *vectors[:4], taps(conv_first)
    )
    below = lax.ppermute(hidden, "space", [((i + 1) % bands, i) for i in range(bands)])
    parts = gather(parts, (20, 21))
    half = ((2, height, columns, channels), BF16)
    keep, send = call(second_kernel, [SMEM] + [VMEM] * 10, [half, half], work)(
        in_smem(plan), length, parts, hidden, below, latent, group_row, *vectors[4:], taps(conv_second),
    )
    got = lax.ppermute(send, "tm", [(i, i ^ 1) for i in range(clips)])
    chips = clips // 2
    got = list(call(spread_kernel, [SMEM] + [VMEM] * 2, [half] * chips)(in_smem(plan), keep, got))
    for step in range(1, chips):
        along = [(i, (i + 2 * step) % clips) for i in range(clips)]
        got[step] = lax.ppermute(got[step], "tm", along)
    (out,) = call(pick_kernel, [SMEM] + [ANY] * chips, [half], [pltpu.SemaphoreType.DMA((2,))], HBM)(in_smem(plan), *got)
    return out


def solution(mesh):
    placed = (P("tm", "space", None, None), P(), P(), P(), P(), P(), P(), P(), P(), P(), P(), P())
    return jax.shard_map(
        local, mesh=mesh, in_specs=placed, out_specs=P("tm", "space", None, None), check_vma=False
    )
```
